512 devices in a mesh: lat: 16 (over x, y_hi), lon: 32 (over z, y_lo, core).
Axes of the slice: x: 4, y: 8 (y_hi: 4, y_lo: 2; y = y_hi * 2 + y_lo), z: 8, core: 2. Of those that a mesh axis runs over, the one named last changes fastest.
Arguments:
- inputs: bfloat16 [512, 512, 256], P('lat', 'lon'), may hold values from -6 to 6
- cotangent: bfloat16 [512, 512, 256], P('lat', 'lon'), may hold values from -6 to 6
- spectral_fine: float32 [32, 64, 2, 256, 256], P('lat', 'lon'), may hold values from -0.25 to 0.25
- spectral_coarse: float32 [16, 32, 2, 256, 256], P('lat', 'lon'), may hold values from -0.25 to 0.25
- weight_in: bfloat16 [256, 1024], replicated, may hold values from -0.375 to 0.375
- weight_out: bfloat16 [1024, 256], replicated, may hold values from -0.1875 to 0.1875
Outputs:
- output: bfloat16 [512, 512, 256], P('lat', 'lon')
- grad_inputs: bfloat16 [512, 512, 256], P('lat', 'lon')
The draws below stay inside these ranges and needn't reach their ends.
All inputs are finite; a program needn't handle non-finite values.
Results may differ from the reference program's by a relative error of at most 0.017.
Values may be sent and summed in bfloat16 or wider, within the bound.
A program may use at most 64 MiB of HBM per device.

```python
import math
from functools import partial
import jax
import jax.numpy as jnp
from jax import lax

C = 256
HID = 1024
ML1 = 32
MW1 = 64
ML2 = 16
MW2 = 32
NLAT = 512
NLON = 512


def level_of(rng, shape, cuts, least, high):
    def one(axis_at, shards_of):
        draws = jax.random.uniform(jax.random.fold_in(jax.random.fold_in(rng, 6), axis_at), (shards_of,), jnp.float32, least / len(cuts), high / len(cuts))
        return jnp.repeat(jnp.exp(draws), shape[axis_at] // shards_of).reshape((-1,) + (1,) * (len(shape) - axis_at - 1))

    level = one(*cuts[0])
    for cut in cuts[1:]:
        level = level * one(*cut)
    return level


def normal_values(key, dims, scale, most, cuts=(), kind=jnp.bfloat16):
    factor_of = level_of(key, dims, cuts, -0.22, 0.18) if cuts else 1.0
    entries = jax.random.normal(key, dims, jnp.float32) * scale * factor_of
    return jnp.minimum(jnp.maximum(entries, -most), most).astype(kind)


def setup_inputs(seed: int = 0) -> dict:
    keys = jax.random.split(jax.random.key(seed), 7)
    inputs = normal_values(keys[0], (NLAT, NLON, C), 1.0, 6.0, ((0, 16), (1, 32)))
    cotangent = normal_values(keys[1], (NLAT, NLON, C), 1.0, 6.0, ((0, 16), (1, 32)))
    spectral_fine = normal_values(keys[2], (ML1, MW1, 2, C, C), (2 * C) ** -0.5, 0.25, ((0, 16), (1, 32)), jnp.float32)
    spectral_coarse = normal_values(keys[3], (ML2, MW2, 2, C, C), (2 * C) ** -0.5, 0.25, ((0, 16), (1, 32)), jnp.float32)
    weight_in = normal_values(keys[4], (C, HID), C ** -0.5, 0.375)
    weight_out = normal_values(keys[5], (HID, C), HID ** -0.5, 0.1875)
    return {"inputs": inputs, "cotangent": cotangent, "spectral_fine": spectral_fine, "spectral_coarse": spectral_coarse, "weight_in": weight_in, "weight_out": weight_out}


highest = lax.Precision.HIGHEST

def mode_table(mode_ids, positions, modulus):
    product = mode_ids[:, None] * positions[None, :] % modulus
    angles = product.astype(jnp.float32) * (2.0 * math.pi / modulus)
    return (jnp.cos(angles), jnp.sin(angles))

def centered(number):
    return jnp.arange(number, dtype=jnp.int32) - number // 2

def lat_forward(grid_field, cos_lat, sin_lat):
    real_part = jnp.einsum('jh,hwc->jwc', cos_lat, grid_field, precision=highest)
    imag_part = -jnp.einsum('jh,hwc->jwc', sin_lat, grid_field, precision=highest)
    return jnp.stack([real_part, imag_part])

def lon_forward(mode_segment, cos_lon, sin_lon):
    real_part = jnp.einsum('kw,jwc->jkc', cos_lon, mode_segment[0], precision=highest) + jnp.einsum('kw,jwc->jkc', sin_lon, mode_segment[1], precision=highest)
    imag_part = jnp.einsum('kw,jwc->jkc', cos_lon, mode_segment[1], precision=highest) - jnp.einsum('kw,jwc->jkc', sin_lon, mode_segment[0], precision=highest)
    return jnp.stack([real_part, imag_part])

def lon_backward(spectrum, cos_lon, sin_lon):
    real_part = jnp.einsum('kw,jko->jwo', cos_lon, spectrum[0], precision=highest) - jnp.einsum('kw,jko->jwo', sin_lon, spectrum[1], precision=highest)
    imag_part = jnp.einsum('kw,jko->jwo', sin_lon, spectrum[0], precision=highest) + jnp.einsum('kw,jko->jwo', cos_lon, spectrum[1], precision=highest)
    return jnp.stack([real_part, imag_part])

def lat_backward(mode_segment, cos_lat, sin_lat):
    return jnp.einsum('jh,jwo->hwo', cos_lat, mode_segment[0], precision=highest) - jnp.einsum('jh,jwo->hwo', sin_lat, mode_segment[1], precision=highest)

def mix_modes(spectrum, weights):
    weight_real = weights[:, :, 0]
    weight_imag = weights[:, :, 1]
    real_part = jnp.einsum('jki,jkio->jko', spectrum[0], weight_real, precision=highest) - jnp.einsum('jki,jkio->jko', spectrum[1], weight_imag, precision=highest)
    imag_part = jnp.einsum('jki,jkio->jko', spectrum[0], weight_imag, precision=highest) + jnp.einsum('jki,jkio->jko', spectrum[1], weight_real, precision=highest)
    return jnp.stack([real_part, imag_part])

def mix_adjoint(spectrum, weights):
    weight_real = weights[:, :, 0]
    weight_imag = weights[:, :, 1]
    real_part = jnp.einsum('jko,jkio->jki', spectrum[0], weight_real, precision=highest) + jnp.einsum('jko,jkio->jki', spectrum[1], weight_imag, precision=highest)
    imag_part = jnp.einsum('jko,jkio->jki', spectrum[1], weight_real, precision=highest) - jnp.einsum('jko,jkio->jki', spectrum[0], weight_imag, precision=highest)
    return jnp.stack([real_part, imag_part])

def shrink(grid_field):
    height, width, depth = grid_field.shape
    return grid_field.reshape(height // 2, 2, width // 2, 2, depth).sum(axis=(1, 3))

def expand(grid_field):
    return jnp.repeat(jnp.repeat(grid_field, 2, axis=0), 2, axis=1)

def feed_forward(mixed, cotangent, weight_in, weight_out):
    hidden = jnp.dot(mixed, weight_in, preferred_element_type=jnp.float32)
    activated, pullback = jax.vjp(partial(jax.nn.gelu, approximate=True), hidden)
    output = (mixed.astype(jnp.float32) + jnp.dot(activated.astype(jnp.bfloat16), weight_out, preferred_element_type=jnp.float32)).astype(jnp.bfloat16)
    d_act = jnp.dot(cotangent, weight_out.T, preferred_element_type=jnp.float32)
    d_hidden = pullback(d_act)[0].astype(jnp.bfloat16)
    d_mixed = (cotangent.astype(jnp.float32) + jnp.dot(d_hidden, weight_in.T, preferred_element_type=jnp.float32)).astype(jnp.bfloat16)
    return (output, d_mixed)

def analysis(grid_field, tables, factor):
    return lon_forward(lat_forward(grid_field, *tables[0]), *tables[1]) * factor

def synthesis(spectrum, tables, factor):
    return lat_backward(lon_backward(spectrum, *tables[1]), *tables[0]) * factor

def reference(inputs, cotangent, spectral_fine, spectral_coarse, weight_in, weight_out):
    fine_tables = (mode_table(centered(ML1), jnp.arange(NLAT, dtype=jnp.int32), NLAT), mode_table(jnp.arange(MW1, dtype=jnp.int32), jnp.arange(NLON, dtype=jnp.int32), NLON))
    coarse_tables = (mode_table(centered(ML2), jnp.arange(NLAT // 2, dtype=jnp.int32), NLAT // 2), mode_table(jnp.arange(MW2, dtype=jnp.int32), jnp.arange(NLON // 2, dtype=jnp.int32), NLON // 2))
    fine_in = 1.0 / math.sqrt(NLAT * NLON)
    fine_out = 1.0 / math.sqrt(ML1 * MW1)
    coarse_in = 1.0 / math.sqrt(NLAT * NLON / 4)
    coarse_out = 1.0 / math.sqrt(ML2 * MW2)
    whole_input = inputs.astype(jnp.float32)
    fine_branch = synthesis(mix_modes(analysis(whole_input, fine_tables, fine_in), spectral_fine), fine_tables, fine_out)
    coarse = shrink(whole_input) * 0.25
    coarse_branch = synthesis(mix_modes(analysis(coarse, coarse_tables, coarse_in), spectral_coarse), coarse_tables, coarse_out)
    mixed = (whole_input + fine_branch + expand(coarse_branch)).astype(jnp.bfloat16)

    def row_step(row_pair):
        return feed_forward(row_pair[0], row_pair[1], weight_in, weight_out)
    output, d_mixed = lax.map(row_step, (mixed, cotangent))
    back_input = d_mixed.astype(jnp.float32)
    back_fine = synthesis(mix_adjoint(analysis(back_input, fine_tables, fine_out), spectral_fine), fine_tables, fine_in)
    back_coarse = synthesis(mix_adjoint(analysis(shrink(back_input), coarse_tables, coarse_out), spectral_coarse), coarse_tables, coarse_in)
    grad_inputs = (back_input + back_fine + 0.25 * expand(back_coarse)).astype(jnp.bfloat16)
    return (output, grad_inputs)
```

```python
from functools import partial
import math

import jax
import jax.numpy as jnp
import numpy as np
from jax import lax
from jax.experimental import pallas as pl
from jax.experimental.pallas import tpu as pltpu
from jax.sharding import PartitionSpec as P

f32 = jnp.float32
bf16 = jnp.bfloat16
MESH = pl.DeviceIdType.MESH
SLOTS = 8
PART = 16


def lon_table(lon_devices, columns):
    table = np.zeros((lon_devices, SLOTS, columns))
    w = np.arange(columns)
    for k in range(lon_devices):
        for b in range(2):
            angle = 2 * np.pi * ((2 * k + b) * w % columns) / columns
            table[k, 2 * b] = np.cos(angle)
            table[k, 2 * b + 1] = -np.sin(angle)
        angle = 2 * np.pi * (k * (w // 2) % (columns // 2)) / (columns // 2)
        table[k, 4] = np.cos(angle)
        table[k, 5] = -np.sin(angle)
    return table.reshape(lon_devices * SLOTS, columns)


def lat_tables(lat_devices, row_count):
    rows = lat_devices * row_count
    g = np.arange(rows).reshape(lat_devices, row_count)
    table = np.zeros((lat_devices, lat_devices, PART, row_count, SLOTS))
    for owner in range(lat_devices):
        for a in range(2):
            p = 2 * owner + a - lat_devices
            angle = 2 * np.pi * (p * g % rows) / rows
            for b in range(2):
                r = 4 * a + 2 * b
                table[:, owner, r, :, 2 * b] = np.cos(angle)
                table[:, owner, r, :, 2 * b + 1] = np.sin(angle)
                table[:, owner, r + 1, :, 2 * b] = -np.sin(angle)
                table[:, owner, r + 1, :, 2 * b + 1] = np.cos(angle)
        p = owner - lat_devices // 2
        angle = 2 * np.pi * (p * (g // 2) % (rows // 2)) / (rows // 2)
        table[:, owner, 8, :, 4] = np.cos(angle)
        table[:, owner, 8, :, 5] = np.sin(angle)
        table[:, owner, 9, :, 4] = -np.sin(angle)
        table[:, owner, 9, :, 5] = np.cos(angle)
    return table.reshape(lat_devices, lat_devices * PART, row_count * SLOTS)


def dot(a, b):
    return jnp.dot(a, b, preferred_element_type=f32)


def dot_t(a, b):
    return lax.dot_general(a, b, (((1,), (1,)), ((), ())), preferred_element_type=f32)


def split_halves(block):
    half = block.shape[1] // 2
    left = block[:, :half].reshape(-1, SLOTS, half)
    right = block[:, half:].reshape(-1, SLOTS, half)
    return jnp.concatenate([left, right], axis=1).astype(bf16)


def join_halves(messages):
    wide = messages.astype(f32)
    joined = jnp.concatenate([wide[:, :SLOTS], wide[:, SLOTS:]], axis=2)
    return joined.reshape(-1, joined.shape[2]).astype(bf16)


def gelu_parts(x):
    c = math.sqrt(2.0 / math.pi)
    square = x * x
    t = jnp.tanh(x * (c + (c * 0.044715) * square))
    half = 0.5 + 0.5 * t
    slope = half + (0.5 * x) * (1.0 - t * t) * (c + (3.0 * c * 0.044715) * square)
    return x * half, slope


def kernel(
    lat_devices, lon_devices, scale, tile,
    x_in, cot_in, fine_in, coarse_in, w_in_in, w_out_in, t_in, tt_in, l_in, lt_in,
    out_ref, grad_ref,
    fine32, coarse32, fine16, coarse16, w_in, w_out, t, tt, l, lt,
    xt, ct, s2, r2, s3, r3, s4, r4, s5, r5, d_act, act, mixed, d_mixed, out_rows, grad_rows,
    load_sem, own_sem, send_lon, recv_lon, send_lat, recv_lat,
):
    i = lax.axis_index("lat")
    k = lax.axis_index("lon")
    columns = lon_devices * 16
    channels = xt.shape[2]

    loads = [
        pltpu.make_async_copy(src, dst, load_sem.at[n])
        for n, (src, dst) in enumerate([
            (t_in, t), (tt_in, tt), (l_in.at[i], l), (lt_in.at[i], lt),
            (fine_in, fine32), (coarse_in, coarse32), (w_in_in, w_in), (w_out_in, w_out),
            (x_in.at[k], xt.at[k]), (cot_in.at[k], ct.at[k]),
        ])
    ]
    for load in loads:
        load.start()

    barrier = pltpu.get_barrier_semaphore()

    def greet_lon(d, _):
        pl.semaphore_signal(
            barrier, inc=1, device_id={"lon": lax.rem(k + d, lon_devices)}, device_id_type=MESH)
        return 0

    def greet_lat(d, _):
        pl.semaphore_signal(
            barrier, inc=1, device_id={"lat": lax.rem(i + d, lat_devices)}, device_id_type=MESH)
        return 0

    lax.fori_loop(1, lon_devices, greet_lon, 0)
    lax.fori_loop(1, lat_devices, greet_lat, 0)
    pl.semaphore_wait(barrier, lon_devices + lat_devices - 2)

    def send_to_lon(stage, source, target):
        def step(d, _):
            other = lax.rem(k + d, lon_devices)
            pltpu.make_async_remote_copy(
                src_ref=source.at[other], dst_ref=target.at[k],
                send_sem=send_lon.at[stage], recv_sem=recv_lon.at[stage],
                device_id={"lon": other}, device_id_type=MESH).start()
            return 0
        lax.fori_loop(1, lon_devices, step, 0)

    def send_to_lat(stage, source, target):
        def step(d, _):
            other = lax.rem(i + d, lat_devices)
            pltpu.make_async_remote_copy(
                src_ref=source.at[other], dst_ref=target.at[i],
                send_sem=send_lat.at[stage], recv_sem=recv_lat.at[stage],
                device_id={"lat": other}, device_id_type=MESH).start()
            return 0
        lax.fori_loop(1, lat_devices, step, 0)

    def spread_to_lat(stage, source, target):
        def step(d, _):
            other = lax.rem(i + d, lat_devices)
            pltpu.make_async_remote_copy(
                src_ref=source, dst_ref=target.at[i],
                send_sem=send_lat.at[stage], recv_sem=recv_lat.at[stage],
                device_id={"lat": other}, device_id_type=MESH).start()
            return 0
        lax.fori_loop(1, lat_devices, step, 0)

    def wait_all(buffer, sem):
        view = buffer.at[pl.ds(0, buffer.shape[0] - 1)]
        pltpu.make_async_copy(view, view, sem).wait()

    send_to_lon(0, x_in, xt)

    for n in range(4):
        loads[n].wait()
    for n in range(4, 8):
        loads[n].wait()
    fine16[...] = fine32[...].astype(bf16)
    coarse16[...] = coarse32[...].astype(bf16)

    def analysis(rows, way):
        s2[way] = split_halves(dot(t[...], rows))
        send_to_lon(1 + 4 * way, s2.at[way], r2.at[way])
        r2[way, k] = s2[way, k]

    def lat_analysis(way):
        wait_all(r2.at[way], recv_lon.at[1 + 4 * way])
        s3[way] = dot(l[...], join_halves(r2[way])).reshape(
            lat_devices, PART, channels).astype(bf16)
        send_to_lat(2 * way, s3.at[way], r3.at[way])
        r3[way, i] = s3[way, i]

    def spectrum(way):
        wait_all(r3.at[way], recv_lat.at[2 * way])
        return r3[way].astype(f32).sum(axis=0) * scale

    def turned(x):
        row = lax.broadcasted_iota(jnp.int32, x.shape, 0)
        up = jnp.concatenate([x[1:], x[:1]], axis=0)
        down = jnp.concatenate([x[-1:], x[:-1]], axis=0)
        return jnp.where(row % 2 == 0, -up, down)

    def mix(x, way):
        y = turned(x)
        x16 = x.astype(bf16)
        y16 = y.astype(bf16)
        row = lax.broadcasted_iota(jnp.int32, x.shape, 0)
        total = jnp.zeros_like(x)
        for m in range(5):
            if m < 4:
                w0 = fine16[m // 2, m % 2, 0]
                w1 = fine16[m // 2, m % 2, 1]
            else:
                w0 = coarse16[0, 0, 0]
                w1 = coarse16[0, 0, 1]
            if way == 0:
                mode = dot(x16, w0) + dot(y16, w1)
            else:
                mode = dot_t(x16, w0) - dot_t(y16, w1)
            total = jnp.where(row // 2 == m, mode, total)
        return total

    def spread(y, way):
        s4[way] = y.astype(bf16)
        spread_to_lat(2 * way + 1, s4.at[way], r4.at[way])
        r4[way, i] = s4[way]

    def lat_synthesis(way):
        wait_all(r4.at[way], recv_lat.at[2 * way + 1])
        s5[way] = split_halves(dot(lt[...], r4[way].reshape(lat_devices * PART, channels)))
        send_to_lon(3 + 3 * way, s5.at[way], r5.at[way])
        r5[way, k] = s5[way, k]

    loads[8].wait()
    wait_all(xt, recv_lon.at[0])
    analysis(xt[...].reshape(columns, channels), 0)
    send_to_lon(2, cot_in, ct)
    lat_analysis(0)
    spread(mix(spectrum(0), 0), 0)

    loads[9].wait()
    wait_all(ct, recv_lon.at[2])
    blocks = tile // 16
    for n in range(columns // tile):
        rows = pl.ds(n * tile, tile)
        cot = ct[pl.ds(n * blocks, blocks)].reshape(tile, channels)
        d_act[rows] = dot_t(cot, w_out[...])

    lat_synthesis(0)
    wait_all(r5.at[0], recv_lon.at[3])
    modes = join_halves(r5[0])
    for n in range(columns // tile):
        rows = pl.ds(n * tile, tile)
        part = pl.ds(n * blocks, blocks)
        x = xt[part].reshape(tile, channels).astype(f32)
        m = (x + dot(tt[rows], modes)).astype(bf16)
        mixed[rows] = m
        value, slope = gelu_parts(dot(m, w_in[...]))
        act[rows] = value.astype(bf16)
        d_hidden = (d_act[rows] * slope).astype(bf16)
        cot = ct[part].reshape(tile, channels).astype(f32)
        d_mixed[rows] = (cot + dot_t(d_hidden, w_in[...])).astype(bf16)

    analysis(d_mixed[...], 1)
    for n in range(columns // tile):
        rows = pl.ds(n * tile, tile)
        value = (mixed[rows].astype(f32) + dot(act[rows], w_out[...])).astype(bf16)
        out_rows[pl.ds(n * blocks, blocks)] = value.reshape(blocks, 16, channels)
    send_to_lon(4, out_rows, out_ref)
    own_out = pltpu.make_async_copy(out_rows.at[k], out_ref.at[k], own_sem.at[0])
    own_out.start()

    lat_analysis(1)
    spread(mix(spectrum(1), 1), 1)
    lat_synthesis(1)
    wait_all(r5.at[1], recv_lon.at[6])
    modes = join_halves(r5[1])
    for n in range(columns // tile):
        rows = pl.ds(n * tile, tile)
        value = (d_mixed[rows].astype(f32) + dot(tt[rows], modes)).astype(bf16)
        grad_rows[pl.ds(n * blocks, blocks)] = value.reshape(blocks, 16, channels)
    send_to_lon(7, grad_rows, grad_ref)
    own_grad = pltpu.make_async_copy(grad_rows.at[k], grad_ref.at[k], own_sem.at[1])
    own_grad.start()

    for stage, buffer in enumerate([
        xt, s2.at[0], ct, s5.at[0], out_rows, s2.at[1], s5.at[1], grad_rows,
    ]):
        wait_all(buffer, send_lon.at[stage])
    for stage, buffer in enumerate([r3.at[0], r4.at[0], r3.at[1], r4.at[1]]):
        wait_all(buffer, send_lat.at[stage])
    wait_all(out_ref, recv_lon.at[4])
    wait_all(grad_ref, recv_lon.at[7])
    own_out.wait()
    own_grad.wait()


def local(t, tt, l, lt, inputs, cotangent, spectral_fine, spectral_coarse, weight_in, weight_out):
    row_count, column_count, channels = inputs.shape
    hidden = weight_in.shape[1]
    lat_devices = lax.axis_size("lat")
    lon_devices = lax.axis_size("lon")
    columns = column_count * lon_devices
    rows = row_count * lat_devices
    assert row_count == lon_devices and column_count == 16
    scale = 1.0 / math.sqrt(rows * columns * 4 * lat_devices * lon_devices)
    tile = min(128, columns)
    half = channels // 2
    lon_message = (2, lon_devices, 2 * SLOTS, half)
    lat_message = (2, lat_devices, PART, channels)
    field = (lon_devices, column_count, channels)
    shape = jax.ShapeDtypeStruct((row_count, column_count, channels), bf16)
    anywhere = pl.BlockSpec(memory_space=pl.ANY)
    scratch = [
        (spectral_fine.shape, f32), (spectral_coarse.shape, f32),
        (spectral_fine.shape, bf16), (spectral_coarse.shape, bf16),
        (weight_in.shape, bf16), (weight_out.shape, bf16),
        (t.shape, bf16), (tt.shape, bf16), (l.shape[1:], bf16), (lt.shape[1:], bf16),
        (field, bf16), (field, bf16),
        (lon_message, bf16), (lon_message, bf16),
        (lat_message, bf16), (lat_message, bf16),
        ((2, PART, channels), bf16), (lat_message, bf16),
        (lon_message, bf16), (lon_message, bf16),
        ((columns, hidden), f32), ((columns, hidden), bf16),
        ((columns, channels), bf16), ((columns, channels), bf16),
        (field, bf16), (field, bf16),
    ]
    return pl.pallas_call(
        partial(kernel, lat_devices, lon_devices, scale, tile),
        out_shape=(shape, shape),
        in_specs=[anywhere] * 10,
        out_specs=(anywhere, anywhere),
        scratch_shapes=[pltpu.VMEM(dims, kind) for dims, kind in scratch] + [
            pltpu.SemaphoreType.DMA((10,)),
            pltpu.SemaphoreType.DMA((2,)),
            pltpu.SemaphoreType.DMA((8,)),
            pltpu.SemaphoreType.DMA((8,)),
            pltpu.SemaphoreType.DMA((4,)),
            pltpu.SemaphoreType.DMA((4,)),
        ],
        compiler_params=pltpu.CompilerParams(
            collective_id=0, has_side_effects=True, vmem_limit_bytes=40 * 1024 * 1024),
    )(inputs, cotangent, spectral_fine, spectral_coarse, weight_in, weight_out, t, tt, l, lt)


def solution(mesh):
    lat_devices, lon_devices = mesh.shape["lat"], mesh.shape["lon"]
    t = lon_table(lon_devices, 16 * lon_devices)
    l = lat_tables(lat_devices, lon_devices)
    tables = [
        np.asarray(table).astype(jnp.bfloat16)
        for table in (t, t.T, l, np.swapaxes(l, 1, 2))
    ]
    field = P("lat", "lon", None)
    modes = P("lat", "lon", None, None, None)
    body = jax.shard_map(
        local,
        mesh=mesh,
        in_specs=(P(), P(), P(), P(), field, field, modes, modes, P(), P()),
        out_specs=(field, field),
        check_vma=False,
    )

    def run(inputs, cotangent, spectral_fine, spectral_coarse, weight_in, weight_out):
        return body(
            *(jnp.asarray(table) for table in tables),
            inputs, cotangent, spectral_fine, spectral_coarse, weight_in, weight_out)

    return run
```

```python
from functools import partial
import math

import jax
import jax.numpy as jnp
import numpy as np
from jax import lax
from jax.experimental import pallas as pl
from jax.experimental.pallas import tpu as pltpu
from jax.sharding import PartitionSpec as P

f32 = jnp.float32
bf16 = jnp.bfloat16
MESH = pl.DeviceIdType.MESH
SLOTS = 8
PART = 16

def lon_table(lon_devices, columns):
    table = np.zeros((lon_devices, SLOTS, columns))
    w = np.arange(columns)
    for k in range(lon_devices):
        for b in range(2):
            angle = 2 * np.pi * ((2 * k + b) * w % columns) / columns
            table[k, 2 * b] = np.cos(angle)
            table[k, 2 * b + 1] = -np.sin(angle)
        angle = 2 * np.pi * (k * (w // 2) % (columns // 2)) / (columns // 2)
        table[k, 4] = np.cos(angle)
        table[k, 5] = -np.sin(angle)
    return table.reshape(lon_devices * SLOTS, columns)

def lat_tables(lat_devices, row_count):
    rows = lat_devices * row_count
    g = np.arange(rows).reshape(lat_devices, row_count)
    table = np.zeros((lat_devices, lat_devices, PART, row_count, SLOTS))
    for owner in range(lat_devices):
        for a in range(2):
            p = 2 * owner + a - lat_devices
            angle = 2 * np.pi * (p * g % rows) / rows
            for b in range(2):
                r = 4 * a + 2 * b
                table[:, owner, r, :, 2 * b] = np.cos(angle)
                table[:, owner, r, :, 2 * b + 1] = np.sin(angle)
                table[:, owner, r + 1, :, 2 * b] = -np.sin(angle)
                table[:, owner, r + 1, :, 2 * b + 1] = np.cos(angle)
        p = owner - lat_devices // 2
        angle = 2 * np.pi * (p * (g // 2) % (rows // 2)) / (rows // 2)
        table[:, owner, 8, :, 4] = np.cos(angle)
        table[:, owner, 8, :, 5] = np.sin(angle)
        table[:, owner, 9, :, 4] = -np.sin(angle)
        table[:, owner, 9, :, 5] = np.cos(angle)
    return table.reshape(lat_devices, lat_devices * PART, row_count * SLOTS)

def dot(a, b):
    return jnp.dot(a, b, preferred_element_type=f32)

def dot_t(a, b):
    return lax.dot_general(a, b, (((1,), (1,)), ((), ())), preferred_element_type=f32)

def split_halves(block):
    half = block.shape[1] // 2
    left = block[:, :half].reshape(-1, SLOTS, half)
    right = block[:, half:].reshape(-1, SLOTS, half)
    return jnp.concatenate([left, right], axis=1).astype(bf16)

def join_halves(messages):
    wide = messages.astype(f32)
    joined = jnp.concatenate([wide[:, :SLOTS], wide[:, SLOTS:]], axis=2)
    return joined.reshape(-1, joined.shape[2]).astype(bf16)

def gelu_parts(x):
    c = math.sqrt(2.0 / math.pi)
    square = x * x
    t = jnp.tanh(x * (c + (c * 0.044715) * square))
    half = 0.5 + 0.5 * t
    slope = half + (0.5 * x) * (1.0 - t * t) * (c + (3.0 * c * 0.044715) * square)
    return x * half, slope

def kernel(
    lat_devices, lon_devices, scale, tile,
    x_in, cot_in, fine_in, coarse_in, w_in_in, w_out_in, t_in, tt_in, l_in, lt_in,
    out_ref, grad_ref,
    fine32, coarse32, fine16, coarse16, w_in, w_out, t, tt, l, lt,
    xt, ct, s2, r2, s3, r3, s4, r4, s5, r5, d_act, act, mixed, d_mixed, out_rows, grad_rows, x_own, cot_own,
    load_sem, own_sem, send_lon, recv_lon, send_lat, recv_lat,
):
    i = lax.axis_index("lat")
    k = lax.axis_index("lon")
    columns = lon_devices * 16
    channels = xt.shape[2]

    loads = [
        pltpu.make_async_copy(src, dst, load_sem.at[n])
        for n, (src, dst) in enumerate([
            (x_in, x_own), (t_in, t), (l_in.at[i], l), (fine_in, fine32), (coarse_in, coarse32),
            (cot_in, cot_own), (lt_in.at[i], lt), (w_out_in, w_out), (tt_in, tt), (w_in_in, w_in),
        ])
    ]
    for load in loads:
        load.start()

    def centre_out(j, n):
        return n // 2 + (j + 1) // 2 * (1 - 2 * (j % 2))

    def lon_partner(j):
        inner = min(4, lon_devices)
        outer = lon_devices // inner
        z = (k // inner + centre_out(j // inner, outer)) % outer
        return z * inner + (k + inner - 1 - j % inner) % inner

    def lat_partner(j):
        inner = min(4, lat_devices)
        outer = lat_devices // inner
        x = (i // inner + centre_out(j % outer, outer)) % outer
        return x * inner + (i + centre_out(j // outer, inner)) % inner

    barrier = pltpu.get_barrier_semaphore()

    def greet_lat(j, _):
        pl.semaphore_signal(
            barrier, inc=1, device_id={"lat": lat_partner(j)}, device_id_type=MESH)
        return 0

    def greet_lon(j, _):
        pl.semaphore_signal(
            barrier, inc=1, device_id={"lon": lon_partner(j)}, device_id_type=MESH)
        return 0

    lax.fori_loop(0, lat_devices - 1, greet_lat, 0)
    lax.fori_loop(0, lon_devices - 1, greet_lon, 0)
    pl.semaphore_wait(barrier, lon_devices + lat_devices - 2)

    pending = []
    arriving = {}

    def send_to_lon(stage, source, target):
        pending.append((target, send_lon.at[stage]))
        arriving['lon', stage] = (target, recv_lon.at[stage])

        def step(j, _):
            other = lon_partner(j)
            pltpu.make_async_remote_copy(
                src_ref=source.at[other], dst_ref=target.at[k],
                send_sem=send_lon.at[stage], recv_sem=recv_lon.at[stage],
                device_id={"lon": other}, device_id_type=MESH).start()
            return 0
        lax.fori_loop(0, lon_devices - 1, step, 0)

    def send_to_lat(stage, source, target, spread=False):
        pending.append((target, send_lat.at[stage]))
        arriving['lat', stage] = (target, recv_lat.at[stage])

        def step(j, _):
            other = lat_partner(j)
            pltpu.make_async_remote_copy(
                src_ref=source if spread else source.at[other], dst_ref=target.at[i],
                send_sem=send_lat.at[stage], recv_sem=recv_lat.at[stage],
                device_id={"lat": other}, device_id_type=MESH).start()
            return 0
        lax.fori_loop(0, lat_devices - 1, step, 0)

    def arrive(group, stage):
        wait_all(*arriving.pop((group, stage)))

    def wait_all(buffer, sem):
        view = buffer.at[pl.ds(0, buffer.shape[0] - 1)]
        pltpu.make_async_copy(view, view, sem).wait()

    opened = dict(enumerate(loads))

    def ready(n):
        opened.pop(n).wait()

    def end():
        for buffer, sem in pending:
            wait_all(buffer, sem)
        for buffer, sem in arriving.values():
            wait_all(buffer, sem)
        for load in opened.values():
            load.wait()

    ready(0)
    send_to_lon(0, x_own, xt)
    xt[k] = x_own[k]

    def analysis(rows, way):
        s2[way] = split_halves(dot(t[...], rows))
        send_to_lon(1 + 4 * way, s2.at[way], r2.at[way])
        r2[way, k] = s2[way, k]

    def lat_analysis(way):
        arrive('lon', 1 + 4 * way)
        s3[way] = dot(l[...], join_halves(r2[way])).reshape(
            lat_devices, PART, channels).astype(bf16)
        send_to_lat(2 * way, s3.at[way], r3.at[way])
        r3[way, i] = s3[way, i]

    def spectrum(way):
        arrive('lat', 2 * way)
        return r3[way].astype(f32).sum(axis=0) * scale

    def turned(x):
        row = lax.broadcasted_iota(jnp.int32, x.shape, 0)
        up = jnp.concatenate([x[1:], x[:1]], axis=0)
        down = jnp.concatenate([x[-1:], x[:-1]], axis=0)
        return jnp.where(row % 2 == 0, -up, down)

    def mix(x, way):
        y = turned(x)
        x16 = x.astype(bf16)
        y16 = y.astype(bf16)
        row = lax.broadcasted_iota(jnp.int32, x.shape, 0)
        total = jnp.zeros_like(x)
        for m in range(5):
            if m < 4:
                w0 = fine16[m // 2, m % 2, 0]
                w1 = fine16[m // 2, m % 2, 1]
            else:
                w0 = coarse16[0, 0, 0]
                w1 = coarse16[0, 0, 1]
            if way == 0:
                mode = dot(x16, w0) + dot(y16, w1)
            else:
                mode = dot_t(x16, w0) - dot_t(y16, w1)
            total = jnp.where(row // 2 == m, mode, total)
        return total

    def spread(y, way):
        s4[way] = y.astype(bf16)
        send_to_lat(2 * way + 1, s4.at[way], r4.at[way], spread=True)
        r4[way, i] = s4[way]

    def lat_synthesis(way):
        arrive('lat', 2 * way + 1)
        s5[way] = split_halves(dot(lt[...], r4[way].reshape(lat_devices * PART, channels)))
        send_to_lon(3 + 3 * way, s5.at[way], r5.at[way])
        r5[way, k] = s5[way, k]

    arrive('lon', 0)

    ready(1)
    analysis(xt[...].reshape(columns, channels), 0)
    for n in (2, 3, 4):
        ready(n)
    fine16[...] = fine32[...].astype(bf16)
    coarse16[...] = coarse32[...].astype(bf16)

    lat_analysis(0)

    ready(5)
    send_to_lon(2, cot_own, ct)
    ct[k] = cot_own[k]
    spread(mix(spectrum(0), 0), 0)

    for n in (6, 7, 8, 9):
        ready(n)
    arrive('lon', 2)
    blocks = tile // 16
    for n in range(columns // tile):
        rows = pl.ds(n * tile, tile)
        cot = ct[pl.ds(n * blocks, blocks)].reshape(tile, channels)
        d_act[rows] = dot_t(cot, w_out[...])

    lat_synthesis(0)

    arrive('lon', 3)
    modes = join_halves(r5[0])
    for n in range(columns // tile):
        rows = pl.ds(n * tile, tile)
        part = pl.ds(n * blocks, blocks)
        x = xt[part].reshape(tile, channels).astype(f32)
        m = (x + dot(tt[rows], modes)).astype(bf16)
        mixed[rows] = m
        value, slope = gelu_parts(dot(m, w_in[...]))
        act[rows] = value.astype(bf16)
        d_hidden = (d_act[rows] * slope).astype(bf16)
        cot = ct[part].reshape(tile, channels).astype(f32)
        d_mixed[rows] = (cot + dot_t(d_hidden, w_in[...])).astype(bf16)

    analysis(d_mixed[...], 1)
    for n in range(columns // tile):
        rows = pl.ds(n * tile, tile)
        value = (mixed[rows].astype(f32) + dot(act[rows], w_out[...])).astype(bf16)
        out_rows[pl.ds(n * blocks, blocks)] = value.reshape(blocks, 16, channels)
    send_to_lon(4, out_rows, out_ref)
    own_out = pltpu.make_async_copy(out_rows.at[k], out_ref.at[k], own_sem.at[0])
    own_out.start()
    opened['out'] = own_out

    lat_analysis(1)

    spread(mix(spectrum(1), 1), 1)

    lat_synthesis(1)

    arrive('lon', 6)
    modes = join_halves(r5[1])
    for n in range(columns // tile):
        rows = pl.ds(n * tile, tile)
        value = (d_mixed[rows].astype(f32) + dot(tt[rows], modes)).astype(bf16)
        grad_rows[pl.ds(n * blocks, blocks)] = value.reshape(blocks, 16, channels)

    send_to_lon(7, grad_rows, grad_ref)
    own_grad = pltpu.make_async_copy(grad_rows.at[k], grad_ref.at[k], own_sem.at[1])
    own_grad.start()
    opened['grad'] = own_grad

    end()

def hand_over(a_in, b_in, a_out, b_out, held, sem):
    arrive = [
        pltpu.make_async_copy(src, held.at[n], sem.at[n]) for n, src in enumerate((a_in, b_in))
    ]
    leave = [
        pltpu.make_async_copy(held.at[n], dst, sem.at[2 + n]) for n, dst in enumerate((a_out, b_out))
    ]
    for copy in arrive:
        copy.start()
    for n in range(2):
        arrive[n].wait()
        leave[n].start()
    for copy in leave:
        copy.wait()

def local(t, tt, l, lt, inputs, cotangent, spectral_fine, spectral_coarse, weight_in, weight_out):
    row_count, column_count, channels = inputs.shape
    hidden = weight_in.shape[1]
    lat_devices = lax.axis_size("lat")
    lon_devices = lax.axis_size("lon")
    columns = column_count * lon_devices
    rows = row_count * lat_devices
    assert row_count == lon_devices and column_count == 16
    scale = 1.0 / math.sqrt(rows * columns * 4 * lat_devices * lon_devices)
    tile = min(128, columns)
    half = channels // 2
    lon_message = (2, lon_devices, 2 * SLOTS, half)
    lat_message = (2, lat_devices, PART, channels)
    field = (lon_devices, column_count, channels)
    shape = jax.ShapeDtypeStruct((row_count, column_count, channels), bf16)
    anywhere = pl.BlockSpec(memory_space=pltpu.HBM)
    scratch = [
        (spectral_fine.shape, f32), (spectral_coarse.shape, f32),
        (spectral_fine.shape, bf16), (spectral_coarse.shape, bf16),
        (weight_in.shape, bf16), (weight_out.shape, bf16),
        (t.shape, bf16), (tt.shape, bf16), (l.shape[1:], bf16), (lt.shape[1:], bf16),
        (field, bf16), (field, bf16),
        (lon_message, bf16), (lon_message, bf16),
        (lat_message, bf16), (lat_message, bf16),
        ((2, PART, channels), bf16), (lat_message, bf16),
        (lon_message, bf16), (lon_message, bf16),
        ((columns, hidden), f32), ((columns, hidden), bf16),
        ((columns, channels), bf16), ((columns, channels), bf16),
        (field, bf16), (field, bf16), (field, bf16), (field, bf16),
    ]
    results = pl.pallas_call(
        partial(kernel, lat_devices, lon_devices, scale, tile),
        out_shape=(shape, shape),
        in_specs=[anywhere] * 10,
        out_specs=(anywhere, anywhere),
        scratch_shapes=[pltpu.VMEM(dims, kind) for dims, kind in scratch] + [
            pltpu.SemaphoreType.DMA((10,)),
            pltpu.SemaphoreType.DMA((2,)),
            pltpu.SemaphoreType.DMA((8,)),
            pltpu.SemaphoreType.DMA((8,)),
            pltpu.SemaphoreType.DMA((4,)),
            pltpu.SemaphoreType.DMA((4,)),
        ],
        compiler_params=pltpu.CompilerParams(
            collective_id=0, has_side_effects=True, vmem_limit_bytes=56 * 1024 * 1024),
    )(inputs, cotangent, spectral_fine, spectral_coarse, weight_in, weight_out, t, tt, l, lt)
    return pl.pallas_call(
        hand_over,
        out_shape=(shape, shape),
        in_specs=[anywhere] * 2,
        out_specs=(anywhere, anywhere),
        scratch_shapes=[pltpu.VMEM((2,) + shape.shape, bf16), pltpu.SemaphoreType.DMA((4,))],
        compiler_params=pltpu.CompilerParams(vmem_limit_bytes=56 * 1024 * 1024),
    )(*results)

def solution(mesh):
    lat_devices, lon_devices = mesh.shape["lat"], mesh.shape["lon"]
    t = lon_table(lon_devices, 16 * lon_devices)
    l = lat_tables(lat_devices, lon_devices)
    tables = [
        np.asarray(table).astype(jnp.bfloat16)
        for table in (t, t.T, l, np.swapaxes(l, 1, 2))
    ]
    field = P("lat", "lon", None)
    modes = P("lat", "lon", None, None, None)
    body = jax.shard_map(
        local,
        mesh=mesh,
        in_specs=(P(), P(), P(), P(), field, field, modes, modes, P(), P()),
        out_specs=(field, field),
        check_vma=False,
    )

    def run(inputs, cotangent, spectral_fine, spectral_coarse, weight_in, weight_out):
        return body(
            *(jnp.asarray(table) for table in tables),
            inputs, cotangent, spectral_fine, spectral_coarse, weight_in, weight_out)

    return run
```

```python
from functools import partial
import math

import jax
import jax.numpy as jnp
import numpy as np
from jax import lax
from jax.experimental import pallas as pl
from jax.experimental.pallas import tpu as pltpu
from jax.sharding import PartitionSpec as P

f32 = jnp.float32
bf16 = jnp.bfloat16
MESH = pl.DeviceIdType.MESH
SLOTS = 8
PART = 16

def lon_table(lon_devices, columns):
    table = np.zeros((lon_devices, SLOTS, columns))
    w = np.arange(columns)
    for k in range(lon_devices):
        for b in range(2):
            angle = 2 * np.pi * ((2 * k + b) * w % columns) / columns
            table[k, 2 * b] = np.cos(angle)
            table[k, 2 * b + 1] = -np.sin(angle)
        angle = 2 * np.pi * (k * (w // 2) % (columns // 2)) / (columns // 2)
        table[k, 4] = np.cos(angle)
        table[k, 5] = -np.sin(angle)
    return table.reshape(lon_devices * SLOTS, columns)

def lat_tables(lat_devices, row_count):
    rows = lat_devices * row_count
    g = np.arange(rows).reshape(lat_devices, row_count)
    table = np.zeros((lat_devices, lat_devices, PART, row_count, SLOTS))
    for owner in range(lat_devices):
        for a in range(2):
            p = 2 * owner + a - lat_devices
            angle = 2 * np.pi * (p * g % rows) / rows
            for b in range(2):
                r = 4 * a + 2 * b
                table[:, owner, r, :, 2 * b] = np.cos(angle)
                table[:, owner, r, :, 2 * b + 1] = np.sin(angle)
                table[:, owner, r + 1, :, 2 * b] = -np.sin(angle)
                table[:, owner, r + 1, :, 2 * b + 1] = np.cos(angle)
        p = owner - lat_devices // 2
        angle = 2 * np.pi * (p * (g // 2) % (rows // 2)) / (rows // 2)
        table[:, owner, 8, :, 4] = np.cos(angle)
        table[:, owner, 8, :, 5] = np.sin(angle)
        table[:, owner, 9, :, 4] = -np.sin(angle)
        table[:, owner, 9, :, 5] = np.cos(angle)
    return table.reshape(lat_devices, lat_devices * PART, row_count * SLOTS)

def dot(a, b):
    return jnp.dot(a, b, preferred_element_type=f32)

def dot_t(a, b):
    return lax.dot_general(a, b, (((1,), (1,)), ((), ())), preferred_element_type=f32)

def split_halves(block):
    half = block.shape[1] // 2
    left = block[:, :half].reshape(-1, SLOTS, half)
    right = block[:, half:].reshape(-1, SLOTS, half)
    return jnp.concatenate([left, right], axis=1).astype(bf16)

def join_halves(messages):
    wide = messages.astype(f32)
    joined = jnp.concatenate([wide[:, :SLOTS], wide[:, SLOTS:]], axis=2)
    return joined.reshape(-1, joined.shape[2]).astype(bf16)

def gelu_parts(x):
    c = math.sqrt(2.0 / math.pi)
    square = x * x
    t = jnp.tanh(x * (c + (c * 0.044715) * square))
    half = 0.5 + 0.5 * t
    slope = half + (0.5 * x) * (1.0 - t * t) * (c + (3.0 * c * 0.044715) * square)
    return x * half, slope

def kernel(
    lat_devices, lon_devices, scale, tile,
    x_in, cot_in, fine_in, coarse_in, w_in_in, w_out_in, t_in, tt_in, l_in, lt_in,
    out_ref, grad_ref,
    fine32, coarse32, fine16, coarse16, w_in, w_out, t, tt, l, lt,
    xt, ct, s2, r2, s3, r3, s4, r4, s5, r5, d_act, act, mixed, d_mixed, out_rows, grad_rows, x_own, cot_own,
    load_sem, own_sem, send_lon, recv_lon, send_lat, recv_lat,
):
    i = lax.axis_index("lat")
    k = lax.axis_index("lon")
    columns = lon_devices * 16
    channels = xt.shape[2]

    loads = [
        pltpu.make_async_copy(src, dst, load_sem.at[n])
        for n, (src, dst) in enumerate([
            (x_in, x_own), (t_in, t), (l_in.at[i], l), (fine_in, fine32), (coarse_in, coarse32),
            (cot_in, cot_own), (lt_in.at[i], lt), (w_out_in, w_out), (tt_in, tt), (w_in_in, w_in),
        ])
    ]
    loads[0].start()

    def centre_out(j, n):
        half = lax.div(j + 1, 2)
        return n // 2 + jnp.where(lax.rem(j, 2) == 0, half, -half)

    lon_inner = min(4, lon_devices)
    lon_outer = lon_devices // lon_inner
    lat_inner = min(4, lat_devices)
    lat_outer = lat_devices // lat_inner
    z_here, x_here = lax.div(k, lon_inner), lax.div(i, lat_inner)

    def lon_partner(j):
        to = lax.rem(z_here + centre_out(lax.div(j, lon_inner), lon_outer), lon_outer)
        return to * lon_inner + lax.rem(k + (lon_inner - 1) - lax.rem(j, lon_inner), lon_inner)

    def lat_partner(j):
        to = lax.rem(x_here + centre_out(lax.rem(j, lat_outer), lat_outer), lat_outer)
        return to * lat_inner + lax.rem(i + centre_out(lax.div(j, lat_outer), lat_inner), lat_inner)

    barrier = pltpu.get_barrier_semaphore()

    def greet_lat(j, _):
        pl.semaphore_signal(
            barrier, inc=1, device_id={"lat": lat_partner(j)}, device_id_type=MESH)
        return 0

    def greet_lon(j, _):
        pl.semaphore_signal(
            barrier, inc=1, device_id={"lon": lon_partner(j)}, device_id_type=MESH)
        return 0

    lax.fori_loop(0, lat_devices - 1, greet_lat, 0)
    lax.fori_loop(0, lon_devices - 1, greet_lon, 0)
    for load in loads[1:]:
        load.start()
    pl.semaphore_wait(barrier, lon_devices + lat_devices - 2)

    pending = []
    arriving = {}

    def send_to_lon(stage, source, target):
        pending.append((target, send_lon.at[stage]))
        arriving['lon', stage] = (target, recv_lon.at[stage])

        def step(j, _):
            other = lon_partner(j)
            pltpu.make_async_remote_copy(
                src_ref=source.at[other], dst_ref=target.at[k],
                send_sem=send_lon.at[stage], recv_sem=recv_lon.at[stage],
                device_id={"lon": other}, device_id_type=MESH).start()
            return 0
        lax.fori_loop(0, lon_devices - 1, step, 0)

    def send_to_lat(stage, source, target, spread=False):
        pending.append((target, send_lat.at[stage]))
        arriving['lat', stage] = (target, recv_lat.at[stage])

        def step(j, _):
            other = lat_partner(j)
            pltpu.make_async_remote_copy(
                src_ref=source if spread else source.at[other], dst_ref=target.at[i],
                send_sem=send_lat.at[stage], recv_sem=recv_lat.at[stage],
                device_id={"lat": other}, device_id_type=MESH).start()
            return 0
        lax.fori_loop(0, lat_devices - 1, step, 0)

    def arrive(group, stage):
        wait_all(*arriving.pop((group, stage)))

    def wait_all(buffer, sem):
        view = buffer.at[pl.ds(0, buffer.shape[0] - 1)]
        pltpu.make_async_copy(view, view, sem).wait()

    opened = dict(enumerate(loads))

    def ready(n):
        opened.pop(n).wait()

    def end():
        for buffer, sem in pending:
            wait_all(buffer, sem)
        for buffer, sem in arriving.values():
            wait_all(buffer, sem)
        for load in opened.values():
            load.wait()

    ready(0)
    send_to_lon(0, x_own, xt)
    xt[k] = x_own[k]

    def analysis(rows, way):
        s2[way] = split_halves(dot(t[...], rows))
        send_to_lon(1 + 4 * way, s2.at[way], r2.at[way])
        r2[way, k] = s2[way, k]

    def lat_analysis(way):
        arrive('lon', 1 + 4 * way)
        s3[way] = dot(l[...], join_halves(r2[way])).reshape(
            lat_devices, PART, channels).astype(bf16)
        send_to_lat(2 * way, s3.at[way], r3.at[way])
        r3[way, i] = s3[way, i]

    def spectrum(way):
        arrive('lat', 2 * way)
        return r3[way].astype(f32).sum(axis=0) * scale

    def turned(x):
        row = lax.broadcasted_iota(jnp.int32, x.shape, 0)
        up = jnp.concatenate([x[1:], x[:1]], axis=0)
        down = jnp.concatenate([x[-1:], x[:-1]], axis=0)
        return jnp.where(row % 2 == 0, -up, down)

    def mix(x, way):
        y = turned(x)
        x16 = x.astype(bf16)
        y16 = y.astype(bf16)
        row = lax.broadcasted_iota(jnp.int32, x.shape, 0)
        total = jnp.zeros_like(x)
        for m in range(5):
            if m < 4:
                w0 = fine16[m // 2, m % 2, 0]
                w1 = fine16[m // 2, m % 2, 1]
            else:
                w0 = coarse16[0, 0, 0]
                w1 = coarse16[0, 0, 1]
            if way == 0:
                mode = dot(x16, w0) + dot(y16, w1)
            else:
                mode = dot_t(x16, w0) - dot_t(y16, w1)
            total = jnp.where(row // 2 == m, mode, total)
        return total

    def spread(y, way):
        s4[way] = y.astype(bf16)
        send_to_lat(2 * way + 1, s4.at[way], r4.at[way], spread=True)
        r4[way, i] = s4[way]

    def lat_synthesis(way):
        arrive('lat', 2 * way + 1)
        s5[way] = split_halves(dot(lt[...], r4[way].reshape(lat_devices * PART, channels)))
        send_to_lon(3 + 3 * way, s5.at[way], r5.at[way])
        r5[way, k] = s5[way, k]

    arrive('lon', 0)

    ready(1)
    analysis(xt[...].reshape(columns, channels), 0)
    for n in (2, 3, 4):
        ready(n)
    fine16[...] = fine32[...].astype(bf16)
    coarse16[...] = coarse32[...].astype(bf16)

    lat_analysis(0)

    ready(5)
    send_to_lon(2, cot_own, ct)
    ct[k] = cot_own[k]
    spread(mix(spectrum(0), 0), 0)

    for n in (6, 7, 8, 9):
        ready(n)
    arrive('lon', 2)
    blocks = tile // 16
    for n in range(columns // tile):
        rows = pl.ds(n * tile, tile)
        cot = ct[pl.ds(n * blocks, blocks)].reshape(tile, channels)
        d_act[rows] = dot_t(cot, w_out[...])

    lat_synthesis(0)

    arrive('lon', 3)
    modes = join_halves(r5[0])
    for n in range(columns // tile):
        rows = pl.ds(n * tile, tile)
        part = pl.ds(n * blocks, blocks)
        x = xt[part].reshape(tile, channels).astype(f32)
        m = (x + dot(tt[rows], modes)).astype(bf16)
        mixed[rows] = m
        value, slope = gelu_parts(dot(m, w_in[...]))
        act[rows] = value.astype(bf16)
        d_hidden = (d_act[rows] * slope).astype(bf16)
        cot = ct[part].reshape(tile, channels).astype(f32)
        d_mixed[rows] = (cot + dot_t(d_hidden, w_in[...])).astype(bf16)

    analysis(d_mixed[...], 1)
    for n in range(columns // tile):
        rows = pl.ds(n * tile, tile)
        value = (mixed[rows].astype(f32) + dot(act[rows], w_out[...])).astype(bf16)
        out_rows[pl.ds(n * blocks, blocks)] = value.reshape(blocks, 16, channels)

    lat_analysis(1)

    send_to_lon(4, out_rows, out_ref)
    own_out = pltpu.make_async_copy(out_rows.at[k], out_ref.at[k], own_sem.at[0])
    own_out.start()
    opened['out'] = own_out

    spread(mix(spectrum(1), 1), 1)

    lat_synthesis(1)

    arrive('lon', 6)
    modes = join_halves(r5[1])
    for n in range(columns // tile):
        rows = pl.ds(n * tile, tile)
        value = (d_mixed[rows].astype(f32) + dot(tt[rows], modes)).astype(bf16)
        grad_rows[pl.ds(n * blocks, blocks)] = value.reshape(blocks, 16, channels)

    send_to_lon(7, grad_rows, grad_ref)
    own_grad = pltpu.make_async_copy(grad_rows.at[k], grad_ref.at[k], own_sem.at[1])
    own_grad.start()
    opened['grad'] = own_grad

    end()

def hand_over(a_in, b_in, a_out, b_out, held, sem):
    arrive = [
        pltpu.make_async_copy(src, held.at[n], sem.at[n]) for n, src in enumerate((a_in, b_in))
    ]
    leave = [
        pltpu.make_async_copy(held.at[n], dst, sem.at[2 + n]) for n, dst in enumerate((a_out, b_out))
    ]
    for copy in arrive:
        copy.start()
    for n in range(2):
        arrive[n].wait()
        leave[n].start()
    for copy in leave:
        copy.wait()

def local(t, tt, l, lt, inputs, cotangent, spectral_fine, spectral_coarse, weight_in, weight_out):
    row_count, column_count, channels = inputs.shape
    hidden = weight_in.shape[1]
    lat_devices = lax.axis_size("lat")
    lon_devices = lax.axis_size("lon")
    columns = column_count * lon_devices
    rows = row_count * lat_devices
    assert row_count == lon_devices and column_count == 16
    scale = 1.0 / math.sqrt(rows * columns * 4 * lat_devices * lon_devices)
    tile = min(128, columns)
    half = channels // 2
    lon_message = (2, lon_devices, 2 * SLOTS, half)
    lat_message = (2, lat_devices, PART, channels)
    field = (lon_devices, column_count, channels)
    shape = jax.ShapeDtypeStruct((row_count, column_count, channels), bf16)
    anywhere = pl.BlockSpec(memory_space=pltpu.HBM)
    scratch = [
        (spectral_fine.shape, f32), (spectral_coarse.shape, f32),
        (spectral_fine.shape, bf16), (spectral_coarse.shape, bf16),
        (weight_in.shape, bf16), (weight_out.shape, bf16),
        (t.shape, bf16), (tt.shape, bf16), (l.shape[1:], bf16), (lt.shape[1:], bf16),
        (field, bf16), (field, bf16),
        (lon_message, bf16), (lon_message, bf16),
        (lat_message, bf16), (lat_message, bf16),
        ((2, PART, channels), bf16), (lat_message, bf16),
        (lon_message, bf16), (lon_message, bf16),
        ((columns, hidden), f32), ((columns, hidden), bf16),
        ((columns, channels), bf16), ((columns, channels), bf16),
        (field, bf16), (field, bf16), (field, bf16), (field, bf16),
    ]
    results = pl.pallas_call(
        partial(kernel, lat_devices, lon_devices, scale, tile),
        out_shape=(shape, shape),
        in_specs=[anywhere] * 10,
        out_specs=(anywhere, anywhere),
        scratch_shapes=[pltpu.VMEM(dims, kind) for dims, kind in scratch] + [
            pltpu.SemaphoreType.DMA((10,)),
            pltpu.SemaphoreType.DMA((2,)),
            pltpu.SemaphoreType.DMA((8,)),
            pltpu.SemaphoreType.DMA((8,)),
            pltpu.SemaphoreType.DMA((4,)),
            pltpu.SemaphoreType.DMA((4,)),
        ],
        compiler_params=pltpu.CompilerParams(
            collective_id=0, has_side_effects=True, vmem_limit_bytes=56 * 1024 * 1024),
    )(inputs, cotangent, spectral_fine, spectral_coarse, weight_in, weight_out, t, tt, l, lt)
    return pl.pallas_call(
        hand_over,
        out_shape=(shape, shape),
        in_specs=[anywhere] * 2,
        out_specs=(anywhere, anywhere),
        scratch_shapes=[pltpu.VMEM((2,) + shape.shape, bf16), pltpu.SemaphoreType.DMA((4,))],
        compiler_params=pltpu.CompilerParams(vmem_limit_bytes=56 * 1024 * 1024),
    )(*results)

def solution(mesh):
    lat_devices, lon_devices = mesh.shape["lat"], mesh.shape["lon"]
    t = lon_table(lon_devices, 16 * lon_devices)
    l = lat_tables(lat_devices, lon_devices)
    tables = [
        np.asarray(table).astype(jnp.bfloat16)
        for table in (t, t.T, l, np.swapaxes(l, 1, 2))
    ]
    field = P("lat", "lon", None)
    modes = P("lat", "lon", None, None, None)
    body = jax.shard_map(
        local,
        mesh=mesh,
        in_specs=(P(), P(), P(), P(), field, field, modes, modes, P(), P()),
        out_specs=(field, field),
        check_vma=False,
    )

    def run(inputs, cotangent, spectral_fine, spectral_coarse, weight_in, weight_out):
        return body(
            *(jnp.asarray(table) for table in tables),
            inputs, cotangent, spectral_fine, spectral_coarse, weight_in, weight_out)

    return run
```

```python
from functools import partial
import math

import jax
import jax.numpy as jnp
import numpy as np
from jax import lax
from jax.experimental import pallas as pl
from jax.experimental.pallas import tpu as pltpu
from jax.sharding import PartitionSpec as P

f32 = jnp.float32
bf16 = jnp.bfloat16
MESH = pl.DeviceIdType.MESH
SLOTS = 8
PART = 16

def lon_table(lon_devices, columns):
    table = np.zeros((lon_devices, SLOTS, columns))
    w = np.arange(columns)
    for k in range(lon_devices):
        for b in range(2):
            angle = 2 * np.pi * ((2 * k + b) * w % columns) / columns
            table[k, 2 * b] = np.cos(angle)
            table[k, 2 * b + 1] = -np.sin(angle)
        angle = 2 * np.pi * (k * (w // 2) % (columns // 2)) / (columns // 2)
        table[k, 4] = np.cos(angle)
        table[k, 5] = -np.sin(angle)
    return table.reshape(lon_devices * SLOTS, columns)

def lat_tables(lat_devices, row_count):
    rows = lat_devices * row_count
    g = np.arange(rows).reshape(lat_devices, row_count)
    table = np.zeros((lat_devices, lat_devices, PART, row_count, SLOTS))
    for owner in range(lat_devices):
        for a in range(2):
            p = 2 * owner + a - lat_devices
            angle = 2 * np.pi * (p * g % rows) / rows
            for b in range(2):
                r = 4 * a + 2 * b
                table[:, owner, r, :, 2 * b] = np.cos(angle)
                table[:, owner, r, :, 2 * b + 1] = np.sin(angle)
                table[:, owner, r + 1, :, 2 * b] = -np.sin(angle)
                table[:, owner, r + 1, :, 2 * b + 1] = np.cos(angle)
        p = owner - lat_devices // 2
        angle = 2 * np.pi * (p * (g // 2) % (rows // 2)) / (rows // 2)
        table[:, owner, 8, :, 4] = np.cos(angle)
        table[:, owner, 8, :, 5] = np.sin(angle)
        table[:, owner, 9, :, 4] = -np.sin(angle)
        table[:, owner, 9, :, 5] = np.cos(angle)
    return table.reshape(lat_devices, lat_devices * PART, row_count * SLOTS)

def dot(a, b):
    return jnp.dot(a, b, preferred_element_type=f32)

def dot_t(a, b):
    return lax.dot_general(a, b, (((1,), (1,)), ((), ())), preferred_element_type=f32)

def split_halves(block):
    half = block.shape[1] // 2
    left = block[:, :half].reshape(-1, SLOTS, half)
    right = block[:, half:].reshape(-1, SLOTS, half)
    return jnp.concatenate([left, right], axis=1).astype(bf16)

def join_halves(messages):
    wide = messages.astype(f32)
    joined = jnp.concatenate([wide[:, :SLOTS], wide[:, SLOTS:]], axis=2)
    return joined.reshape(-1, joined.shape[2]).astype(bf16)

def gelu_parts(x):
    c = math.sqrt(2.0 / math.pi)
    square = x * x
    t = jnp.tanh(x * (c + (c * 0.044715) * square))
    half = 0.5 + 0.5 * t
    slope = half + (0.5 * x) * (1.0 - t * t) * (c + (3.0 * c * 0.044715) * square)
    return x * half, slope

def kernel(
    lat_devices, lon_devices, scale, tile,
    x_in, cot_in, fine_in, coarse_in, w_in_in, w_out_in, t_in, tt_in, l_in, lt_in,
    out_ref, grad_ref,
    fine32, coarse32, fine16, coarse16, w_in, w_out, t, tt, l, lt,
    xt, ct, s2, r2, s3, r3, s4, r4, s5, r5, d_act, act, mixed, d_mixed, out_rows, grad_rows, x_own, cot_own,
    load_sem, own_sem, send_lon, recv_lon, send_lat, recv_lat,
):
    i = lax.axis_index("lat")
    k = lax.axis_index("lon")
    columns = lon_devices * 16
    channels = xt.shape[2]

    loads = [
        pltpu.make_async_copy(src, dst, load_sem.at[n])
        for n, (src, dst) in enumerate([
            (x_in, x_own), (t_in, t), (l_in.at[i], l), (fine_in, fine32), (coarse_in, coarse32),
            (cot_in, cot_own), (lt_in.at[i], lt), (w_out_in, w_out), (tt_in, tt), (w_in_in, w_in),
        ])
    ]
    loads[0].start()

    def centre_out(j, n):
        half = lax.div(j + 1, 2)
        return n // 2 + jnp.where(lax.rem(j, 2) == 0, half, -half)

    lon_inner = min(4, lon_devices)
    lon_outer = lon_devices // lon_inner
    lat_inner = min(4, lat_devices)
    lat_outer = lat_devices // lat_inner
    z_here, x_here = lax.div(k, lon_inner), lax.div(i, lat_inner)

    def lon_partner(j):
        to = lax.rem(z_here + centre_out(lax.div(j, lon_inner), lon_outer), lon_outer)
        return to * lon_inner + lax.rem(k + (lon_inner - 1) - lax.rem(j, lon_inner), lon_inner)

    def lat_partner(j):
        to = lax.rem(x_here + centre_out(lax.rem(j, lat_outer), lat_outer), lat_outer)
        return to * lat_inner + lax.rem(i + centre_out(lax.div(j, lat_outer), lat_inner), lat_inner)

    barrier = pltpu.get_barrier_semaphore()

    def greet_lat(j, _):
        pl.semaphore_signal(
            barrier, inc=1, device_id={"lat": lat_partner(j)}, device_id_type=MESH)
        return 0

    def greet_lon(j, _):
        pl.semaphore_signal(
            barrier, inc=1, device_id={"lon": lon_partner(j)}, device_id_type=MESH)
        return 0

    lax.fori_loop(0, lat_devices - 1, greet_lat, 0)
    lax.fori_loop(0, lon_devices - 1, greet_lon, 0)
    for load in loads[1:]:
        load.start()
    pl.semaphore_wait(barrier, lon_devices + lat_devices - 2)

    pending = []
    arriving = {}

    def send_to_lon(stage, source, target):
        pending.append((target, send_lon.at[stage]))
        arriving['lon', stage] = (target, recv_lon.at[stage])

        def step(j, _):
            other = lon_partner(j)
            pltpu.make_async_remote_copy(
                src_ref=source.at[other], dst_ref=target.at[k],
                send_sem=send_lon.at[stage], recv_sem=recv_lon.at[stage],
                device_id={"lon": other}, device_id_type=MESH).start()
            return 0
        lax.fori_loop(0, lon_devices - 1, step, 0)

    def send_to_lat(stage, source, target, spread=False):
        pending.append((target, send_lat.at[stage]))
        arriving['lat', stage] = (target, recv_lat.at[stage])

        def step(j, _):
            other = lat_partner(j)
            pltpu.make_async_remote_copy(
                src_ref=source if spread else source.at[other], dst_ref=target.at[i],
                send_sem=send_lat.at[stage], recv_sem=recv_lat.at[stage],
                device_id={"lat": other}, device_id_type=MESH).start()
            return 0
        lax.fori_loop(0, lat_devices - 1, step, 0)

    def arrive(group, stage):
        wait_all(*arriving.pop((group, stage)))

    def wait_all(buffer, sem):
        view = buffer.at[pl.ds(0, buffer.shape[0] - 1)]
        pltpu.make_async_copy(view, view, sem).wait()

    opened = dict(enumerate(loads))

    def ready(n):
        opened.pop(n).wait()

    def end():
        for buffer, sem in pending:
            wait_all(buffer, sem)
        for buffer, sem in arriving.values():
            wait_all(buffer, sem)
        for load in opened.values():
            load.wait()

    ready(0)
    send_to_lon(0, x_own, xt)
    xt[k] = x_own[k]

    def analysis(rows, way):
        s2[way] = split_halves(dot(t[...], rows))
        send_to_lon(1 + 4 * way, s2.at[way], r2.at[way])
        r2[way, k] = s2[way, k]

    def lat_analysis(way):
        arrive('lon', 1 + 4 * way)
        s3[way] = dot(l[...], join_halves(r2[way])).reshape(
            lat_devices, PART, channels).astype(bf16)
        send_to_lat(2 * way, s3.at[way], r3.at[way])
        r3[way, i] = s3[way, i]

    def spectrum(way):
        arrive('lat', 2 * way)
        return r3[way].astype(f32).sum(axis=0) * scale

    def turned(x):
        row = lax.broadcasted_iota(jnp.int32, x.shape, 0)
        up = jnp.concatenate([x[1:], x[:1]], axis=0)
        down = jnp.concatenate([x[-1:], x[:-1]], axis=0)
        return jnp.where(row % 2 == 0, -up, down)

    def mix(x, way):
        y = turned(x)
        x16 = x.astype(bf16)
        y16 = y.astype(bf16)
        row = lax.broadcasted_iota(jnp.int32, x.shape, 0)
        total = jnp.zeros_like(x)
        for m in range(5):
            if m < 4:
                w0 = fine16[m // 2, m % 2, 0]
                w1 = fine16[m // 2, m % 2, 1]
            else:
                w0 = coarse16[0, 0, 0]
                w1 = coarse16[0, 0, 1]
            if way == 0:
                mode = dot(x16, w0) + dot(y16, w1)
            else:
                mode = dot_t(x16, w0) - dot_t(y16, w1)
            total = jnp.where(row // 2 == m, mode, total)
        return total

    def spread(y, way):
        s4[way] = y.astype(bf16)
        send_to_lat(2 * way + 1, s4.at[way], r4.at[way], spread=True)
        r4[way, i] = s4[way]

    def lat_synthesis(way):
        arrive('lat', 2 * way + 1)
        s5[way] = split_halves(dot(lt[...], r4[way].reshape(lat_devices * PART, channels)))
        send_to_lon(3 + 3 * way, s5.at[way], r5.at[way])
        r5[way, k] = s5[way, k]

    arrive('lon', 0)

    ready(1)
    analysis(xt[...].reshape(columns, channels), 0)
    for n in (2, 3, 4):
        ready(n)
    fine16[...] = fine32[...].astype(bf16)
    coarse16[...] = coarse32[...].astype(bf16)

    lat_analysis(0)

    ready(5)
    send_to_lon(2, cot_own, ct)
    ct[k] = cot_own[k]
    spread(mix(spectrum(0), 0), 0)

    for n in (6, 7, 8, 9):
        ready(n)
    arrive('lon', 2)
    blocks = tile // 16
    for n in range(columns // tile):
        rows = pl.ds(n * tile, tile)
        cot = ct[pl.ds(n * blocks, blocks)].reshape(tile, channels)
        d_act[rows] = dot_t(cot, w_out[...])

    lat_synthesis(0)

    arrive('lon', 3)
    modes = join_halves(r5[0])
    for n in range(columns // tile):
        rows = pl.ds(n * tile, tile)
        part = pl.ds(n * blocks, blocks)
        x = xt[part].reshape(tile, channels).astype(f32)
        m = (x + dot(tt[rows], modes)).astype(bf16)
        mixed[rows] = m
        value, slope = gelu_parts(dot(m, w_in[...]))
        act[rows] = value.astype(bf16)
        d_hidden = (d_act[rows] * slope).astype(bf16)
        cot = ct[part].reshape(tile, channels).astype(f32)
        d_mixed[rows] = (cot + dot_t(d_hidden, w_in[...])).astype(bf16)

    analysis(d_mixed[...], 1)
    for n in range(columns // tile):
        rows = pl.ds(n * tile, tile)
        value = (mixed[rows].astype(f32) + dot(act[rows], w_out[...])).astype(bf16)
        out_rows[pl.ds(n * blocks, blocks)] = value.reshape(blocks, 16, channels)

    lat_analysis(1)

    send_to_lon(4, out_rows, out_ref)
    own_out = pltpu.make_async_copy(out_rows.at[k], out_ref.at[k], own_sem.at[0])
    own_out.start()
    opened['out'] = own_out

    spread(mix(spectrum(1), 1), 1)

    lat_synthesis(1)

    arrive('lon', 6)
    modes = join_halves(r5[1])
    for n in range(columns // tile):
        rows = pl.ds(n * tile, tile)
        value = (d_mixed[rows].astype(f32) + dot(tt[rows], modes)).astype(bf16)
        grad_rows[pl.ds(n * blocks, blocks)] = value.reshape(blocks, 16, channels)

    send_to_lon(7, grad_rows, grad_ref)
    own_grad = pltpu.make_async_copy(grad_rows.at[k], grad_ref.at[k], own_sem.at[1])
    own_grad.start()
    opened['grad'] = own_grad

    end()

def hand_over(a_in, b_in, a_out, b_out, sem):
    leave = [
        pltpu.make_async_copy(src, dst, sem.at[n])
        for n, (src, dst) in enumerate(((a_in, a_out), (b_in, b_out)))
    ]
    for copy in leave:
        copy.start()
    for copy in leave:
        copy.wait()

def local(t, tt, l, lt, inputs, cotangent, spectral_fine, spectral_coarse, weight_in, weight_out):
    row_count, column_count, channels = inputs.shape
    hidden = weight_in.shape[1]
    lat_devices = lax.axis_size("lat")
    lon_devices = lax.axis_size("lon")
    columns = column_count * lon_devices
    rows = row_count * lat_devices
    assert row_count == lon_devices and column_count == 16
    scale = 1.0 / math.sqrt(rows * columns * 4 * lat_devices * lon_devices)
    tile = min(512, columns)
    half = channels // 2
    lon_message = (2, lon_devices, 2 * SLOTS, half)
    lat_message = (2, lat_devices, PART, channels)
    field = (lon_devices, column_count, channels)
    shape = jax.ShapeDtypeStruct((row_count, column_count, channels), bf16)
    anywhere = pl.BlockSpec(memory_space=pltpu.HBM)
    scratch = [
        (spectral_fine.shape, f32), (spectral_coarse.shape, f32),
        (spectral_fine.shape, bf16), (spectral_coarse.shape, bf16),
        (weight_in.shape, bf16), (weight_out.shape, bf16),
        (t.shape, bf16), (tt.shape, bf16), (l.shape[1:], bf16), (lt.shape[1:], bf16),
        (field, bf16), (field, bf16),
        (lon_message, bf16), (lon_message, bf16),
        (lat_message, bf16), (lat_message, bf16),
        ((2, PART, channels), bf16), (lat_message, bf16),
        (lon_message, bf16), (lon_message, bf16),
        ((columns, hidden), f32), ((columns, hidden), bf16),
        ((columns, channels), bf16), ((columns, channels), bf16),
        (field, bf16), (field, bf16), (field, bf16), (field, bf16),
    ]
    results = pl.pallas_call(
        partial(kernel, lat_devices, lon_devices, scale, tile),
        out_shape=(pltpu.VMEM(shape.shape, bf16), pltpu.VMEM(shape.shape, bf16)),
        in_specs=[anywhere] * 10,
        out_specs=(pl.BlockSpec(memory_space=pl.ANY),) * 2,
        scratch_shapes=[pltpu.VMEM(dims, kind) for dims, kind in scratch] + [
            pltpu.SemaphoreType.DMA((10,)),
            pltpu.SemaphoreType.DMA((2,)),
            pltpu.SemaphoreType.DMA((8,)),
            pltpu.SemaphoreType.DMA((8,)),
            pltpu.SemaphoreType.DMA((4,)),
            pltpu.SemaphoreType.DMA((4,)),
        ],
        compiler_params=pltpu.CompilerParams(
            collective_id=0, has_side_effects=True, vmem_limit_bytes=56 * 1024 * 1024),
    )(inputs, cotangent, spectral_fine, spectral_coarse, weight_in, weight_out, t, tt, l, lt)
    return pl.pallas_call(
        hand_over,
        out_shape=(shape, shape),
        in_specs=[pl.BlockSpec(memory_space=pl.ANY)] * 2,
        out_specs=(anywhere, anywhere),
        scratch_shapes=[pltpu.SemaphoreType.DMA((2,))],
        compiler_params=pltpu.CompilerParams(vmem_limit_bytes=1024 * 1024),
    )(*results)

def solution(mesh):
    lat_devices, lon_devices = mesh.shape["lat"], mesh.shape["lon"]
    t = lon_table(lon_devices, 16 * lon_devices)
    l = lat_tables(lat_devices, lon_devices)
    tables = [
        np.asarray(table).astype(jnp.bfloat16)
        for table in (t, t.T, l, np.swapaxes(l, 1, 2))
    ]
    field = P("lat", "lon", None)
    modes = P("lat", "lon", None, None, None)
    body = jax.shard_map(
        local,
        mesh=mesh,
        in_specs=(P(), P(), P(), P(), field, field, modes, modes, P(), P()),
        out_specs=(field, field),
        check_vma=False,
    )

    def run(inputs, cotangent, spectral_fine, spectral_coarse, weight_in, weight_out):
        return body(
            *(jnp.asarray(table) for table in tables),
            inputs, cotangent, spectral_fine, spectral_coarse, weight_in, weight_out)

    return run
```

```python
from functools import partial
import math

import jax
import jax.numpy as jnp
import numpy as np
from jax import lax
from jax.experimental import pallas as pl
from jax.experimental.pallas import tpu as pltpu
from jax.sharding import PartitionSpec as P

f32 = jnp.float32
bf16 = jnp.bfloat16
MESH = pl.DeviceIdType.MESH
SLOTS = 8
PART = 16

def lon_table(lon_devices, columns):
    table = np.zeros((lon_devices, SLOTS, columns))
    w = np.arange(columns)
    for k in range(lon_devices):
        for b in range(2):
            angle = 2 * np.pi * ((2 * k + b) * w % columns) / columns
            table[k, 2 * b] = np.cos(angle)
            table[k, 2 * b + 1] = -np.sin(angle)
        angle = 2 * np.pi * (k * (w // 2) % (columns // 2)) / (columns // 2)
        table[k, 4] = np.cos(angle)
        table[k, 5] = -np.sin(angle)
    return table.reshape(lon_devices * SLOTS, columns)

def lat_tables(lat_devices, row_count):
    rows = lat_devices * row_count
    g = np.arange(rows).reshape(lat_devices, row_count)
    table = np.zeros((lat_devices, lat_devices, PART, row_count, SLOTS))
    for owner in range(lat_devices):
        for a in range(2):
            p = 2 * owner + a - lat_devices
            angle = 2 * np.pi * (p * g % rows) / rows
            for b in range(2):
                r = 4 * a + 2 * b
                table[:, owner, r, :, 2 * b] = np.cos(angle)
                table[:, owner, r, :, 2 * b + 1] = np.sin(angle)
                table[:, owner, r + 1, :, 2 * b] = -np.sin(angle)
                table[:, owner, r + 1, :, 2 * b + 1] = np.cos(angle)
        p = owner - lat_devices // 2
        angle = 2 * np.pi * (p * (g // 2) % (rows // 2)) / (rows // 2)
        table[:, owner, 8, :, 4] = np.cos(angle)
        table[:, owner, 8, :, 5] = np.sin(angle)
        table[:, owner, 9, :, 4] = -np.sin(angle)
        table[:, owner, 9, :, 5] = np.cos(angle)
    return table.reshape(lat_devices, lat_devices * PART, row_count * SLOTS)

def dot(a, b):
    return jnp.dot(a, b, preferred_element_type=f32)

def dot_t(a, b):
    return lax.dot_general(a, b, (((1,), (1,)), ((), ())), preferred_element_type=f32)

def split_halves(block):
    half = block.shape[1] // 2
    left = block[:, :half].reshape(-1, SLOTS, half)
    right = block[:, half:].reshape(-1, SLOTS, half)
    return jnp.concatenate([left, right], axis=1).astype(bf16)

def join_halves(messages):
    wide = messages.astype(f32)
    joined = jnp.concatenate([wide[:, :SLOTS], wide[:, SLOTS:]], axis=2)
    return joined.reshape(-1, joined.shape[2]).astype(bf16)

def gelu_parts(x):
    c = math.sqrt(2.0 / math.pi)
    square = x * x
    t = jnp.tanh(x * (c + (c * 0.044715) * square))
    half = 0.5 + 0.5 * t
    slope = half + (0.5 * x) * (1.0 - t * t) * (c + (3.0 * c * 0.044715) * square)
    return x * half, slope

def kernel(
    lat_devices, lon_devices, scale, tile,
    x_in, cot_in, fine_in, coarse_in, w_in_in, w_out_in, t_in, tt_in, l_in, lt_in,
    out_ref, grad_ref,
    fine32, coarse32, fine16, coarse16, w_in, w_out, t, tt, l, lt,
    xt, ct, s2, r2, s3, r3, s4, r4, s5, r5, d_act, act, mixed, d_mixed, out_rows, grad_rows, x_own, cot_own,
    load_sem, own_sem, send_lon, recv_lon, send_lat, recv_lat,
):
    i = lax.axis_index("lat")
    k = lax.axis_index("lon")
    columns = lon_devices * 16
    channels = xt.shape[2]

    loads = [
        pltpu.make_async_copy(src, dst, load_sem.at[n])
        for n, (src, dst) in enumerate([
            (x_in, x_own), (t_in, t), (l_in.at[i], l), (fine_in, fine32), (coarse_in, coarse32),
            (cot_in, cot_own), (lt_in.at[i], lt), (w_out_in, w_out), (tt_in, tt), (w_in_in, w_in),
        ])
    ]
    loads[0].start()

    def centre_out(j, n):
        half = lax.div(j + 1, 2)
        return n // 2 + jnp.where(lax.rem(j, 2) == 0, half, -half)

    lon_inner = min(4, lon_devices)
    lon_outer = lon_devices // lon_inner
    lat_inner = min(4, lat_devices)
    lat_outer = lat_devices // lat_inner
    z_here, x_here = lax.div(k, lon_inner), lax.div(i, lat_inner)

    def lon_partner(j):
        to = lax.rem(z_here + centre_out(lax.div(j, lon_inner), lon_outer), lon_outer)
        return to * lon_inner + lax.rem(k + (lon_inner - 1) - lax.rem(j, lon_inner), lon_inner)

    def lat_partner(j):
        to = lax.rem(x_here + centre_out(lax.rem(j, lat_outer), lat_outer), lat_outer)
        return to * lat_inner + lax.rem(i + centre_out(lax.div(j, lat_outer), lat_inner), lat_inner)

    barrier = pltpu.get_barrier_semaphore()

    def greet_lat(j, _):
        pl.semaphore_signal(
            barrier, inc=1, device_id={"lat": lat_partner(j)}, device_id_type=MESH)
        return 0

    def greet_lon(j, _):
        pl.semaphore_signal(
            barrier, inc=1, device_id={"lon": lon_partner(j)}, device_id_type=MESH)
        return 0

    lax.fori_loop(0, lat_devices - 1, greet_lat, 0)
    lax.fori_loop(0, lon_devices - 1, greet_lon, 0)
    for load in loads[1:]:
        load.start()
    pl.semaphore_wait(barrier, lon_devices + lat_devices - 2)

    pending = []
    arriving = {}

    def send_to_lon(stage, source, target):
        pending.append((target, send_lon.at[stage]))
        arriving['lon', stage] = (target, recv_lon.at[stage])

        def step(j, _):
            other = lon_partner(j)
            pltpu.make_async_remote_copy(
                src_ref=source.at[other], dst_ref=target.at[k],
                send_sem=send_lon.at[stage], recv_sem=recv_lon.at[stage],
                device_id={"lon": other}, device_id_type=MESH).start()
            return 0
        lax.fori_loop(0, lon_devices - 1, step, 0)

    def send_to_lat(stage, source, target, spread=False):
        pending.append((target, send_lat.at[stage]))
        arriving['lat', stage] = (target, recv_lat.at[stage])

        def step(j, _):
            other = lat_partner(j)
            pltpu.make_async_remote_copy(
                src_ref=source if spread else source.at[other], dst_ref=target.at[i],
                send_sem=send_lat.at[stage], recv_sem=recv_lat.at[stage],
                device_id={"lat": other}, device_id_type=MESH).start()
            return 0
        lax.fori_loop(0, lat_devices - 1, step, 0)

    def arrive(group, stage):
        wait_all(*arriving.pop((group, stage)))

    def wait_all(buffer, sem):
        view = buffer.at[pl.ds(0, buffer.shape[0] - 1)]
        pltpu.make_async_copy(view, view, sem).wait()

    opened = dict(enumerate(loads))

    def ready(n):
        opened.pop(n).wait()

    def end():
        for buffer, sem in pending:
            wait_all(buffer, sem)
        for buffer, sem in arriving.values():
            wait_all(buffer, sem)
        for load in opened.values():
            load.wait()

    ready(0)
    send_to_lon(0, x_own, xt)
    xt[k] = x_own[k]

    def analysis(rows, way):
        s2[way] = split_halves(dot(t[...], rows))
        send_to_lon(1 + 4 * way, s2.at[way], r2.at[way])
        r2[way, k] = s2[way, k]

    def lat_analysis(way):
        arrive('lon', 1 + 4 * way)
        s3[way] = dot(l[...], join_halves(r2[way])).reshape(
            lat_devices, PART, channels).astype(bf16)
        send_to_lat(2 * way, s3.at[way], r3.at[way])
        r3[way, i] = s3[way, i]

    def spectrum(way):
        arrive('lat', 2 * way)
        return r3[way].astype(f32).sum(axis=0) * scale

    def turned(x):
        row = lax.broadcasted_iota(jnp.int32, x.shape, 0)
        up = jnp.concatenate([x[1:], x[:1]], axis=0)
        down = jnp.concatenate([x[-1:], x[:-1]], axis=0)
        return jnp.where(row % 2 == 0, -up, down)

    def mix(x, way):
        y = turned(x)
        x16 = x.astype(bf16)
        y16 = y.astype(bf16)
        row = lax.broadcasted_iota(jnp.int32, x.shape, 0)
        total = jnp.zeros_like(x)
        for m in range(5):
            if m < 4:
                w0 = fine16[m // 2, m % 2, 0]
                w1 = fine16[m // 2, m % 2, 1]
            else:
                w0 = coarse16[0, 0, 0]
                w1 = coarse16[0, 0, 1]
            if way == 0:
                mode = dot(x16, w0) + dot(y16, w1)
            else:
                mode = dot_t(x16, w0) - dot_t(y16, w1)
            total = jnp.where(row // 2 == m, mode, total)
        return total

    def spread(y, way):
        s4[way] = y.astype(bf16)
        send_to_lat(2 * way + 1, s4.at[way], r4.at[way], spread=True)
        r4[way, i] = s4[way]

    def lat_synthesis(way):
        arrive('lat', 2 * way + 1)
        s5[way] = split_halves(dot(lt[...], r4[way].reshape(lat_devices * PART, channels)))
        send_to_lon(3 + 3 * way, s5.at[way], r5.at[way])
        r5[way, k] = s5[way, k]

    arrive('lon', 0)

    ready(1)
    analysis(xt[...].reshape(columns, channels), 0)
    for n in (2, 3, 4):
        ready(n)
    fine16[...] = fine32[...].astype(bf16)
    coarse16[...] = coarse32[...].astype(bf16)

    lat_analysis(0)

    ready(5)
    send_to_lon(2, cot_own, ct)
    ct[k] = cot_own[k]
    spread(mix(spectrum(0), 0), 0)

    for n in (6, 7, 8, 9):
        ready(n)
    arrive('lon', 2)
    blocks = tile // 16
    for n in range(columns // tile):
        rows = pl.ds(n * tile, tile)
        cot = ct[pl.ds(n * blocks, blocks)].reshape(tile, channels)
        d_act[rows] = dot_t(cot, w_out[...])

    lat_synthesis(0)

    arrive('lon', 3)
    modes = join_halves(r5[0])
    x = xt[...].reshape(columns, channels).astype(f32)
    m = (x + dot(tt[...], modes)).astype(bf16)
    mixed[...] = m
    value, slope = gelu_parts(dot(m, w_in[...]))
    act[...] = value.astype(bf16)
    d_hidden = (d_act[...] * slope).astype(bf16)
    cot = ct[...].reshape(columns, channels).astype(f32)
    d_mixed[...] = (cot + dot_t(d_hidden, w_in[...])).astype(bf16)

    analysis(d_mixed[...], 1)
    for n in range(columns // tile):
        rows = pl.ds(n * tile, tile)
        value = (mixed[rows].astype(f32) + dot(act[rows], w_out[...])).astype(bf16)
        out_rows[pl.ds(n * blocks, blocks)] = value.reshape(blocks, 16, channels)

    lat_analysis(1)

    send_to_lon(4, out_rows, out_ref)
    own_out = pltpu.make_async_copy(out_rows.at[k], out_ref.at[k], own_sem.at[0])
    own_out.start()
    opened['out'] = own_out

    spread(mix(spectrum(1), 1), 1)

    lat_synthesis(1)

    arrive('lon', 6)
    modes = join_halves(r5[1])
    pending.append((grad_ref, send_lon.at[7]))
    arriving['lon', 7] = (grad_ref, recv_lon.at[7])
    chunks = max(1, lon_outer // 2)
    share = lon_devices // chunks
    for j in range(chunks):
        away = chunks // 2 + (j + 1) // 2 * (1 - 2 * (j % 2))
        first = lax.rem(lax.div(k, share) + away, chunks) * share
        rows = pl.ds(pl.multiple_of(first * 16, share * 16), share * 16)
        value = (d_mixed[rows].astype(f32) + dot(tt[rows], modes)).astype(bf16)
        grad_rows[pl.ds(first, share)] = value.reshape(share, 16, channels)

        def step(n, _):
            other = first + n

            @pl.when(other != k)
            def _():
                pltpu.make_async_remote_copy(
                    src_ref=grad_rows.at[other], dst_ref=grad_ref.at[k],
                    send_sem=send_lon.at[7], recv_sem=recv_lon.at[7],
                    device_id={"lon": other}, device_id_type=MESH).start()
            return 0
        lax.fori_loop(0, share, step, 0)
    own_grad = pltpu.make_async_copy(grad_rows.at[k], grad_ref.at[k], own_sem.at[1])
    own_grad.start()
    opened['grad'] = own_grad

    end()

def hand_over(a_in, b_in, a_out, b_out, sem):
    leave = [
        pltpu.make_async_copy(src, dst, sem.at[n])
        for n, (src, dst) in enumerate(((a_in, a_out), (b_in, b_out)))
    ]
    for copy in leave:
        copy.start()
    for copy in leave:
        copy.wait()

def local(t, tt, l, lt, inputs, cotangent, spectral_fine, spectral_coarse, weight_in, weight_out):
    row_count, column_count, channels = inputs.shape
    hidden = weight_in.shape[1]
    lat_devices = lax.axis_size("lat")
    lon_devices = lax.axis_size("lon")
    columns = column_count * lon_devices
    rows = row_count * lat_devices
    assert row_count == lon_devices and column_count == 16
    scale = 1.0 / math.sqrt(rows * columns * 4 * lat_devices * lon_devices)
    tile = min(128, columns)
    half = channels // 2
    lon_message = (2, lon_devices, 2 * SLOTS, half)
    lat_message = (2, lat_devices, PART, channels)
    field = (lon_devices, column_count, channels)
    shape = jax.ShapeDtypeStruct((row_count, column_count, channels), bf16)
    anywhere = pl.BlockSpec(memory_space=pltpu.HBM)
    scratch = [
        (spectral_fine.shape, f32), (spectral_coarse.shape, f32),
        (spectral_fine.shape, bf16), (spectral_coarse.shape, bf16),
        (weight_in.shape, bf16), (weight_out.shape, bf16),
        (t.shape, bf16), (tt.shape, bf16), (l.shape[1:], bf16), (lt.shape[1:], bf16),
        (field, bf16), (field, bf16),
        (lon_message, bf16), (lon_message, bf16),
        (lat_message, bf16), (lat_message, bf16),
        ((2, PART, channels), bf16), (lat_message, bf16),
        (lon_message, bf16), (lon_message, bf16),
        ((columns, hidden), f32), ((columns, hidden), bf16),
        ((columns, channels), bf16), ((columns, channels), bf16),
        (field, bf16), (field, bf16), (field, bf16), (field, bf16),
    ]
    results = pl.pallas_call(
        partial(kernel, lat_devices, lon_devices, scale, tile),
        out_shape=(pltpu.VMEM(shape.shape, bf16), pltpu.VMEM(shape.shape, bf16)),
        in_specs=[anywhere] * 10,
        out_specs=(pl.BlockSpec(memory_space=pl.ANY),) * 2,
        scratch_shapes=[pltpu.VMEM(dims, kind) for dims, kind in scratch] + [
            pltpu.SemaphoreType.DMA((10,)),
            pltpu.SemaphoreType.DMA((2,)),
            pltpu.SemaphoreType.DMA((8,)),
            pltpu.SemaphoreType.DMA((8,)),
            pltpu.SemaphoreType.DMA((4,)),
            pltpu.SemaphoreType.DMA((4,)),
        ],
        compiler_params=pltpu.CompilerParams(
            collective_id=0, has_side_effects=True, vmem_limit_bytes=56 * 1024 * 1024),
    )(inputs, cotangent, spectral_fine, spectral_coarse, weight_in, weight_out, t, tt, l, lt)
    return pl.pallas_call(
        hand_over,
        out_shape=(shape, shape),
        in_specs=[pl.BlockSpec(memory_space=pl.ANY)] * 2,
        out_specs=(anywhere, anywhere),
        scratch_shapes=[pltpu.SemaphoreType.DMA((2,))],
        compiler_params=pltpu.CompilerParams(vmem_limit_bytes=1024 * 1024),
    )(*results)

def solution(mesh):
    lat_devices, lon_devices = mesh.shape["lat"], mesh.shape["lon"]
    t = lon_table(lon_devices, 16 * lon_devices)
    l = lat_tables(lat_devices, lon_devices)
    tables = [
        np.asarray(table).astype(jnp.bfloat16)
        for table in (t, t.T, l, np.swapaxes(l, 1, 2))
    ]
    field = P("lat", "lon", None)
    modes = P("lat", "lon", None, None, None)
    body = jax.shard_map(
        local,
        mesh=mesh,
        in_specs=(P(), P(), P(), P(), field, field, modes, modes, P(), P()),
        out_specs=(field, field),
        check_vma=False,
    )

    def run(inputs, cotangent, spectral_fine, spectral_coarse, weight_in, weight_out):
        return body(
            *(jnp.asarray(table) for table in tables),
            inputs, cotangent, spectral_fine, spectral_coarse, weight_in, weight_out)

    return run
```

```python
from functools import partial
import math

import jax
import jax.numpy as jnp
import numpy as np
from jax import lax
from jax.experimental import pallas as pl
from jax.experimental.pallas import tpu as pltpu
from jax.sharding import PartitionSpec as P

f32 = jnp.float32
bf16 = jnp.bfloat16
MESH = pl.DeviceIdType.MESH
SLOTS = 8
PART = 16

def lon_table(lon_devices, columns):
    table = np.zeros((lon_devices, SLOTS, columns))
    w = np.arange(columns)
    for k in range(lon_devices):
        for b in range(2):
            angle = 2 * np.pi * ((2 * k + b) * w % columns) / columns
            table[k, 2 * b] = np.cos(angle)
            table[k, 2 * b + 1] = -np.sin(angle)
        angle = 2 * np.pi * (k * (w // 2) % (columns // 2)) / (columns // 2)
        table[k, 4] = np.cos(angle)
        table[k, 5] = -np.sin(angle)
    return table.reshape(lon_devices * SLOTS, columns)

def lat_tables(lat_devices, row_count):
    rows = lat_devices * row_count
    g = np.arange(rows).reshape(lat_devices, row_count)
    table = np.zeros((lat_devices, lat_devices, PART, row_count, SLOTS))
    for owner in range(lat_devices):
        for a in range(2):
            p = 2 * owner + a - lat_devices
            angle = 2 * np.pi * (p * g % rows) / rows
            for b in range(2):
                r = 4 * a + 2 * b
                table[:, owner, r, :, 2 * b] = np.cos(angle)
                table[:, owner, r, :, 2 * b + 1] = np.sin(angle)
                table[:, owner, r + 1, :, 2 * b] = -np.sin(angle)
                table[:, owner, r + 1, :, 2 * b + 1] = np.cos(angle)
        p = owner - lat_devices // 2
        angle = 2 * np.pi * (p * (g // 2) % (rows // 2)) / (rows // 2)
        table[:, owner, 8, :, 4] = np.cos(angle)
        table[:, owner, 8, :, 5] = np.sin(angle)
        table[:, owner, 9, :, 4] = -np.sin(angle)
        table[:, owner, 9, :, 5] = np.cos(angle)
    return table.reshape(lat_devices, lat_devices * PART, row_count * SLOTS)

def dot(a, b):
    return jnp.dot(a, b, preferred_element_type=f32)

def dot_t(a, b):
    return lax.dot_general(a, b, (((1,), (1,)), ((), ())), preferred_element_type=f32)

def split_halves(block):
    half = block.shape[1] // 2
    left = block[:, :half].reshape(-1, SLOTS, half)
    right = block[:, half:].reshape(-1, SLOTS, half)
    return jnp.concatenate([left, right], axis=1).astype(bf16)

def join_halves(messages):
    wide = messages.astype(f32)
    joined = jnp.concatenate([wide[:, :SLOTS], wide[:, SLOTS:]], axis=2)
    return joined.reshape(-1, joined.shape[2]).astype(bf16)

def gelu_parts(x):
    c = math.sqrt(2.0 / math.pi)
    square = x * x
    t = jnp.tanh(x * (c + (c * 0.044715) * square))
    half = 0.5 + 0.5 * t
    slope = half + (0.5 * x) * (1.0 - t * t) * (c + (3.0 * c * 0.044715) * square)
    return x * half, slope

def kernel(
    lat_devices, lon_devices, scale, tile,
    x_in, cot_in, fine_in, coarse_in, w_in_in, w_out_in, t_in, tt_in, l_in, lt_in,
    out_ref, grad_ref,
    fine32, coarse32, fine16, coarse16, w_in, w_out, t, tt, l, lt,
    xt, ct, s2, r2, s3, r3, s4, r4, s5, r5, d_act, act, mixed, d_mixed, out_rows, grad_rows, x_own, cot_own,
    load_sem, own_sem, send_lon, recv_lon, send_lat, recv_lat,
):
    i = lax.axis_index("lat")
    k = lax.axis_index("lon")
    columns = lon_devices * 16
    channels = xt.shape[2]

    loads = [
        pltpu.make_async_copy(src, dst, load_sem.at[n])
        for n, (src, dst) in enumerate([
            (x_in, x_own), (t_in, t), (l_in.at[i], l), (fine_in, fine32), (coarse_in, coarse32),
            (cot_in, cot_own), (lt_in.at[i], lt), (w_out_in, w_out), (tt_in, tt), (w_in_in, w_in),
        ])
    ]
    loads[0].start()

    def centre_out(j, n):
        half = lax.div(j + 1, 2)
        return n // 2 + jnp.where(lax.rem(j, 2) == 0, half, -half)

    lon_inner = min(4, lon_devices)
    lon_outer = lon_devices // lon_inner
    lat_inner = min(4, lat_devices)
    lat_outer = lat_devices // lat_inner
    z_here, x_here = lax.div(k, lon_inner), lax.div(i, lat_inner)

    def lon_partner(j):
        to = lax.rem(z_here + centre_out(lax.div(j, lon_inner), lon_outer), lon_outer)
        return to * lon_inner + lax.rem(k + (lon_inner - 1) - lax.rem(j, lon_inner), lon_inner)

    def lat_partner(j):
        to = lax.rem(x_here + centre_out(lax.rem(j, lat_outer), lat_outer), lat_outer)
        return to * lat_inner + lax.rem(i + centre_out(lax.div(j, lat_outer), lat_inner), lat_inner)

    barrier = pltpu.get_barrier_semaphore()

    def greet_lat(j, _):
        pl.semaphore_signal(
            barrier, inc=1, device_id={"lat": lat_partner(j)}, device_id_type=MESH)
        return 0

    def greet_lon(j, _):
        pl.semaphore_signal(
            barrier, inc=1, device_id={"lon": lon_partner(j)}, device_id_type=MESH)
        return 0

    lax.fori_loop(0, lat_devices - 1, greet_lat, 0, unroll=True)
    lax.fori_loop(0, lon_devices - 1, greet_lon, 0, unroll=True)
    for load in loads[1:]:
        load.start()
    pl.semaphore_wait(barrier, lon_devices + lat_devices - 2)

    pending = []
    arriving = {}

    def send_to_lon(stage, source, target):
        pending.append((target, send_lon.at[stage]))
        arriving['lon', stage] = (target, recv_lon.at[stage])

        def step(j, _):
            other = lon_partner(j)
            pltpu.make_async_remote_copy(
                src_ref=source.at[other], dst_ref=target.at[k],
                send_sem=send_lon.at[stage], recv_sem=recv_lon.at[stage],
                device_id={"lon": other}, device_id_type=MESH).start()
            return 0
        lax.fori_loop(0, lon_devices - 1, step, 0)

    def send_to_lat(stage, source, target, spread=False):
        pending.append((target, send_lat.at[stage]))
        arriving['lat', stage] = (target, recv_lat.at[stage])

        def step(j, _):
            other = lat_partner(j)
            pltpu.make_async_remote_copy(
                src_ref=source if spread else source.at[other], dst_ref=target.at[i],
                send_sem=send_lat.at[stage], recv_sem=recv_lat.at[stage],
                device_id={"lat": other}, device_id_type=MESH).start()
            return 0
        lax.fori_loop(0, lat_devices - 1, step, 0)

    def arrive(group, stage):
        wait_all(*arriving.pop((group, stage)))

    def wait_all(buffer, sem):
        view = buffer.at[pl.ds(0, buffer.shape[0] - 1)]
        pltpu.make_async_copy(view, view, sem).wait()

    opened = dict(enumerate(loads))

    def ready(n):
        opened.pop(n).wait()

    def end():
        for buffer, sem in pending:
            wait_all(buffer, sem)
        for buffer, sem in arriving.values():
            wait_all(buffer, sem)
        for load in opened.values():
            load.wait()

    ready(0)
    send_to_lon(0, x_own, xt)
    xt[k] = x_own[k]

    def analysis(rows, way):
        s2[way] = split_halves(dot(t[...], rows))
        send_to_lon(1 + 4 * way, s2.at[way], r2.at[way])
        r2[way, k] = s2[way, k]

    def lat_analysis(way):
        arrive('lon', 1 + 4 * way)
        s3[way] = dot(l[...], join_halves(r2[way])).reshape(
            lat_devices, PART, channels).astype(bf16)
        send_to_lat(2 * way, s3.at[way], r3.at[way])
        r3[way, i] = s3[way, i]

    def spectrum(way):
        arrive('lat', 2 * way)
        return r3[way].astype(f32).sum(axis=0) * scale

    def turned(x):
        row = lax.broadcasted_iota(jnp.int32, x.shape, 0)
        up = jnp.concatenate([x[1:], x[:1]], axis=0)
        down = jnp.concatenate([x[-1:], x[:-1]], axis=0)
        return jnp.where(row % 2 == 0, -up, down)

    def mix(x, way):
        y = turned(x)
        x16 = x.astype(bf16)
        y16 = y.astype(bf16)
        row = lax.broadcasted_iota(jnp.int32, x.shape, 0)
        total = jnp.zeros_like(x)
        for m in range(5):
            if m < 4:
                w0 = fine16[m // 2, m % 2, 0]
                w1 = fine16[m // 2, m % 2, 1]
            else:
                w0 = coarse16[0, 0, 0]
                w1 = coarse16[0, 0, 1]
            if way == 0:
                mode = dot(x16, w0) + dot(y16, w1)
            else:
                mode = dot_t(x16, w0) - dot_t(y16, w1)
            total = jnp.where(row // 2 == m, mode, total)
        return total

    def spread(y, way):
        s4[way] = y.astype(bf16)
        send_to_lat(2 * way + 1, s4.at[way], r4.at[way], spread=True)
        r4[way, i] = s4[way]

    def lat_synthesis(way):
        arrive('lat', 2 * way + 1)
        s5[way] = split_halves(dot(lt[...], r4[way].reshape(lat_devices * PART, channels)))
        send_to_lon(3 + 3 * way, s5.at[way], r5.at[way])
        r5[way, k] = s5[way, k]

    arrive('lon', 0)

    ready(1)
    analysis(xt[...].reshape(columns, channels), 0)
    for n in (2, 3, 4):
        ready(n)
    fine16[...] = fine32[...].astype(bf16)
    coarse16[...] = coarse32[...].astype(bf16)

    lat_analysis(0)

    ready(5)
    send_to_lon(2, cot_own, ct)
    ct[k] = cot_own[k]
    spread(mix(spectrum(0), 0), 0)

    for n in (6, 7, 8, 9):
        ready(n)
    arrive('lon', 2)
    blocks = tile // 16
    for n in range(columns // tile):
        rows = pl.ds(n * tile, tile)
        cot = ct[pl.ds(n * blocks, blocks)].reshape(tile, channels)
        d_act[rows] = dot_t(cot, w_out[...])

    lat_synthesis(0)

    arrive('lon', 3)
    modes = join_halves(r5[0])
    x = xt[...].reshape(columns, channels).astype(f32)
    m = (x + dot(tt[...], modes)).astype(bf16)
    mixed[...] = m
    value, slope = gelu_parts(dot(m, w_in[...]))
    act[...] = value.astype(bf16)
    d_hidden = (d_act[...] * slope).astype(bf16)
    cot = ct[...].reshape(columns, channels).astype(f32)
    d_mixed[...] = (cot + dot_t(d_hidden, w_in[...])).astype(bf16)

    analysis(d_mixed[...], 1)
    for n in range(columns // tile):
        rows = pl.ds(n * tile, tile)
        value = (mixed[rows].astype(f32) + dot(act[rows], w_out[...])).astype(bf16)
        out_rows[pl.ds(n * blocks, blocks)] = value.reshape(blocks, 16, channels)

    lat_analysis(1)

    send_to_lon(4, out_rows, out_ref)
    own_out = pltpu.make_async_copy(out_rows.at[k], out_ref.at[k], own_sem.at[0])
    own_out.start()
    opened['out'] = own_out

    spread(mix(spectrum(1), 1), 1)

    lat_synthesis(1)

    arrive('lon', 6)
    modes = join_halves(r5[1])
    pending.append((grad_ref, send_lon.at[7]))
    arriving['lon', 7] = (grad_ref, recv_lon.at[7])
    chunks = max(1, lon_outer // 2)
    share = lon_devices // chunks
    for j in range(chunks):
        away = chunks // 2 + (j + 1) // 2 * (1 - 2 * (j % 2))
        first = lax.rem(lax.div(k, share) + away, chunks) * share
        rows = pl.ds(pl.multiple_of(first * 16, share * 16), share * 16)
        value = (d_mixed[rows].astype(f32) + dot(tt[rows], modes)).astype(bf16)
        grad_rows[pl.ds(first, share)] = value.reshape(share, 16, channels)

        def step(n, _):
            other = first + n

            @pl.when(other != k)
            def _():
                pltpu.make_async_remote_copy(
                    src_ref=grad_rows.at[other], dst_ref=grad_ref.at[k],
                    send_sem=send_lon.at[7], recv_sem=recv_lon.at[7],
                    device_id={"lon": other}, device_id_type=MESH).start()
            return 0
        lax.fori_loop(0, share, step, 0)
    own_grad = pltpu.make_async_copy(grad_rows.at[k], grad_ref.at[k], own_sem.at[1])
    own_grad.start()
    opened['grad'] = own_grad

    end()

def hand_over(a_in, b_in, a_out, b_out, sem):
    leave = [
        pltpu.make_async_copy(src, dst, sem.at[n])
        for n, (src, dst) in enumerate(((a_in, a_out), (b_in, b_out)))
    ]
    for copy in leave:
        copy.start()
    for copy in leave:
        copy.wait()

def local(t, tt, l, lt, inputs, cotangent, spectral_fine, spectral_coarse, weight_in, weight_out):
    row_count, column_count, channels = inputs.shape
    hidden = weight_in.shape[1]
    lat_devices = lax.axis_size("lat")
    lon_devices = lax.axis_size("lon")
    columns = column_count * lon_devices
    rows = row_count * lat_devices
    assert row_count == lon_devices and column_count == 16
    scale = 1.0 / math.sqrt(rows * columns * 4 * lat_devices * lon_devices)
    tile = min(128, columns)
    half = channels // 2
    lon_message = (2, lon_devices, 2 * SLOTS, half)
    lat_message = (2, lat_devices, PART, channels)
    field = (lon_devices, column_count, channels)
    shape = jax.ShapeDtypeStruct((row_count, column_count, channels), bf16)
    anywhere = pl.BlockSpec(memory_space=pltpu.HBM)
    scratch = [
        (spectral_fine.shape, f32), (spectral_coarse.shape, f32),
        (spectral_fine.shape, bf16), (spectral_coarse.shape, bf16),
        (weight_in.shape, bf16), (weight_out.shape, bf16),
        (t.shape, bf16), (tt.shape, bf16), (l.shape[1:], bf16), (lt.shape[1:], bf16),
        (field, bf16), (field, bf16),
        (lon_message, bf16), (lon_message, bf16),
        (lat_message, bf16), (lat_message, bf16),
        ((2, PART, channels), bf16), (lat_message, bf16),
        (lon_message, bf16), (lon_message, bf16),
        ((columns, hidden), f32), ((columns, hidden), bf16),
        ((columns, channels), bf16), ((columns, channels), bf16),
        (field, bf16), (field, bf16), (field, bf16), (field, bf16),
    ]
    results = pl.pallas_call(
        partial(kernel, lat_devices, lon_devices, scale, tile),
        out_shape=(pltpu.VMEM(shape.shape, bf16), pltpu.VMEM(shape.shape, bf16)),
        in_specs=[anywhere] * 10,
        out_specs=(pl.BlockSpec(memory_space=pl.ANY),) * 2,
        scratch_shapes=[pltpu.VMEM(dims, kind) for dims, kind in scratch] + [
            pltpu.SemaphoreType.DMA((10,)),
            pltpu.SemaphoreType.DMA((2,)),
            pltpu.SemaphoreType.DMA((8,)),
            pltpu.SemaphoreType.DMA((8,)),
            pltpu.SemaphoreType.DMA((4,)),
            pltpu.SemaphoreType.DMA((4,)),
        ],
        compiler_params=pltpu.CompilerParams(
            collective_id=0, has_side_effects=True, vmem_limit_bytes=56 * 1024 * 1024),
    )(inputs, cotangent, spectral_fine, spectral_coarse, weight_in, weight_out, t, tt, l, lt)
    return pl.pallas_call(
        hand_over,
        out_shape=(shape, shape),
        in_specs=[pl.BlockSpec(memory_space=pl.ANY)] * 2,
        out_specs=(anywhere, anywhere),
        scratch_shapes=[pltpu.SemaphoreType.DMA((2,))],
        compiler_params=pltpu.CompilerParams(vmem_limit_bytes=1024 * 1024),
    )(*results)

def solution(mesh):
    lat_devices, lon_devices = mesh.shape["lat"], mesh.shape["lon"]
    t = lon_table(lon_devices, 16 * lon_devices)
    l = lat_tables(lat_devices, lon_devices)
    tables = [
        np.asarray(table).astype(jnp.bfloat16)
        for table in (t, t.T, l, np.swapaxes(l, 1, 2))
    ]
    field = P("lat", "lon", None)
    modes = P("lat", "lon", None, None, None)
    body = jax.shard_map(
        local,
        mesh=mesh,
        in_specs=(P(), P(), P(), P(), field, field, modes, modes, P(), P()),
        out_specs=(field, field),
        check_vma=False,
    )

    def run(inputs, cotangent, spectral_fine, spectral_coarse, weight_in, weight_out):
        return body(
            *(jnp.asarray(table) for table in tables),
            inputs, cotangent, spectral_fine, spectral_coarse, weight_in, weight_out)

    return run
```
